256 devices in a mesh: users: 32 (over y, z), dims: 8 (over x, core).
Axes of the slice: x: 4, y: 4, z: 8, core: 2. Of those that a mesh axis runs over, the one named last changes fastest.
Arguments:
- user_factors: bfloat16 [65536, 1024], P('users', 'dims'), may hold values from -1.08 to 1.08
- item_factors: bfloat16 [4096, 1024], P('users', 'dims'), may hold values from -1.08 to 1.08
- ratings: bfloat16 [960, 256, 256], P('users'), may hold values from -6 to 6
- tile_coords: int32 [960, 2], P('users'), may hold values from 0 to 15, as said below
- tile_count: int32 [32], P('users'), may hold values from 1 to 30, as said below
- item_gram: bfloat16 [1024, 1024], P(None, 'dims'), as said below
- user_gram: bfloat16 [1024, 1024], P(None, 'dims'), as said below
- user_inverse: float32 [1024, 128], P('dims')
- item_inverse: float32 [1024, 128], P('dims')
Outputs:
- user_new: bfloat16 [65536, 1024], P('users', 'dims')
- item_new: bfloat16 [4096, 1024], P('users', 'dims')
The draws below stay inside these ranges and needn't reach their ends.
Inputs may be any that keep to these rules, and one draw needn't show every extreme that they name: `tile_coords`: within one slab's 30 slots no pair (tile row, item panel) repeats; column 0 is below 8, column 1 below 16. `tile_count`: some slab has exactly 30 tiles. `item_gram`: Symmetric. `user_gram`: Symmetric.
All inputs are finite; a program needn't handle non-finite values.
Results may differ from the reference program's by a relative error of at most 0.014.
Values may be sent and summed in bfloat16 or wider, within the bound.
A program may use at most 64 MiB of HBM per device.

```python
import math
import jax
import jax.numpy as jnp
from jax import lax

BLK = 128
TILE = 256
USR_DEV = 2048
ITM_DEV = 128
TPD = 30
RANK = 1024
USERS = 65536
ITEMS = 4096
N_USERS = 32
N_DIMS = 8


def slab_orders(key):
    slab_keys = jax.random.split(key, N_USERS)
    pair_count = USR_DEV // TILE * (ITM_DEV * N_USERS // TILE)
    return jax.vmap(lambda slab_key: jax.random.permutation(slab_key, pair_count)[:TPD])(slab_keys)


def factor_table(key, row_count):
    value_key = jax.random.fold_in(key, 0)
    values = 0.18 * jax.random.normal(value_key, (row_count, N_DIMS * BLK), jnp.float32)
    return jnp.clip(values, -1.08, 1.08)


def draw_user_factors(key, part):
    key = jax.random.fold_in(key, 17)
    return factor_table(key, USR_DEV * N_USERS).astype(jnp.bfloat16)


def draw_item_factors(key, part):
    key = jax.random.fold_in(key, 18)
    return factor_table(key, ITM_DEV * N_USERS).astype(jnp.bfloat16)


def draw_ratings(key, part):
    key = jax.random.fold_in(key, 19)
    shape = (TPD * N_USERS, TILE, TILE)
    values = jnp.clip(jax.random.normal(key, shape, jnp.float32), -6.0, 6.0)
    return values.astype(jnp.bfloat16)


def draw_tile_coords(key, part):
    key = jax.random.fold_in(key, 11)
    orders = slab_orders(key).reshape(N_USERS * TPD).astype(jnp.int32)
    panel_count = ITM_DEV * N_USERS // TILE
    return jnp.stack([orders // panel_count, orders % panel_count], axis=1).astype(jnp.int32)


def draw_tile_count(key, part):
    key = jax.random.fold_in(key, 12)
    count_key, full_key = jax.random.split(key)
    counts = jax.random.randint(count_key, (N_USERS,), 1, TPD + 1)
    fullest = jax.random.randint(full_key, (), 0, N_USERS)
    return jnp.where(jnp.arange(N_USERS) == fullest, TPD, counts).astype(jnp.int32)


def symmetric_gram(key, level, spread, coupling):
    diag_key, noise_key = jax.random.split(key)
    width = N_DIMS * BLK
    index = jnp.arange(width)
    on_diagonal = (index[:, None] == index[None, :]).astype(jnp.float32)
    scales = level * jnp.exp(jax.random.uniform(diag_key, (width,), minval=-spread, maxval=spread))
    noise = jax.random.normal(noise_key, (width, width), jnp.float32)
    mixed = (noise + noise.T) * (coupling / math.sqrt(width))
    return on_diagonal * scales[:, None] + mixed * (1.0 - on_diagonal)


def draw_item_gram(key, part):
    key = jax.random.fold_in(key, 13)
    return symmetric_gram(key, 0.03, 0.7, 0.0106).astype(jnp.bfloat16)


def draw_user_gram(key, part):
    key = jax.random.fold_in(key, 14)
    return symmetric_gram(key, 0.5, 0.6, 0.08).astype(jnp.bfloat16)


def block_inverse(key, level):
    diag_key, noise_key = jax.random.split(key)
    width = N_DIMS * BLK
    row_in_block = jnp.arange(width) % BLK
    on_diagonal = (row_in_block[:, None] == jnp.arange(BLK)[None, :]).astype(jnp.float32)
    diag_scale = jax.random.uniform(diag_key, (width, 1), minval=0.7, maxval=1.3)
    noise = jax.random.normal(noise_key, (width, BLK), jnp.float32) * (0.4 / math.sqrt(BLK))
    return level * (on_diagonal * diag_scale + noise)


def draw_user_inverse(key, part):
    key = jax.random.fold_in(key, 15)
    return block_inverse(key, 0.05)


def draw_item_inverse(key, part):
    key = jax.random.fold_in(key, 16)
    return block_inverse(key, 0.0077)


def setup_inputs(seed: int = 0) -> dict:
    arg_keys = jax.random.split(jax.random.key(seed), 10)
    return {
        "user_factors": draw_user_factors(jax.random.fold_in(arg_keys[9], 71), 0),
        "item_factors": draw_item_factors(jax.random.fold_in(arg_keys[9], 71), 0),
        "ratings": draw_ratings(jax.random.fold_in(arg_keys[9], 71), 0),
        "tile_coords": draw_tile_coords(jax.random.fold_in(arg_keys[9], 71), 0),
        "tile_count": draw_tile_count(jax.random.fold_in(arg_keys[9], 71), 0),
        "item_gram": draw_item_gram(jax.random.fold_in(arg_keys[9], 71), 0),
        "user_gram": draw_user_gram(jax.random.fold_in(arg_keys[9], 71), 0),
        "user_inverse": draw_user_inverse(jax.random.fold_in(arg_keys[9], 71), 0),
        "item_inverse": draw_item_inverse(jax.random.fold_in(arg_keys[9], 71), 0),
    }


UNOBSERVED = 256.0
REGULAR = 2.0
HIGHEST = lax.Precision.HIGHEST


def tile_rows(source_table, starts):
    offsets = starts.astype(jnp.int32)[:, None] * TILE + jnp.arange(TILE, dtype=jnp.int32)[None, :]
    return source_table[offsets]


def predict(user_tiles, item_tiles):
    totals = jnp.zeros((user_tiles.shape[0], TILE, TILE), jnp.float32)
    for factor_block in range(N_DIMS):
        lower = factor_block * BLK
        partial_value = jnp.einsum("sik,sjk->sij", user_tiles[:, :, lower:lower + BLK].astype(jnp.float32), item_tiles[:, :, lower:lower + BLK].astype(jnp.float32))
        rounded = lax.optimization_barrier(partial_value.astype(jnp.bfloat16))
        totals = totals + rounded.astype(jnp.float32)
    return totals


def newton(factors, gradient, inverse):
    row_count = gradient.shape[0]
    update = jnp.einsum("mcb,cbk->mck", gradient.reshape(row_count, N_DIMS, BLK), inverse.reshape(N_DIMS, BLK, BLK), precision=HIGHEST)
    return (factors.astype(jnp.float32) + update.reshape(row_count, RANK)).astype(jnp.bfloat16)


def reference(user_factors, item_factors, ratings, tile_coords, tile_count, item_gram, user_gram, user_inverse, item_inverse):
    coords = tile_coords.reshape(N_USERS, TPD, 2)
    rating_tiles = ratings.reshape(N_USERS, TPD, TILE, TILE)
    slot_ids = jnp.arange(TPD, dtype=jnp.int32)

    def user_slab(packed):
        slab_rows, slab_coords, slab_ratings, slab_count = packed
        live_mask = (slot_ids < slab_count).astype(jnp.float32)[:, None, None]
        user_tiles = tile_rows(slab_rows, slab_coords[:, 0])
        item_tiles = tile_rows(item_factors, slab_coords[:, 1])
        errors = (live_mask * (slab_ratings.astype(jnp.float32) - predict(user_tiles, item_tiles))).astype(jnp.bfloat16)
        additions = jnp.einsum("sij,sjk->sik", errors.astype(jnp.float32), item_tiles.astype(jnp.float32))
        observed = jnp.zeros((USR_DEV // TILE, TILE, RANK), jnp.float32).at[slab_coords[:, 0]].add(additions)
        gradient = observed.reshape(USR_DEV, RANK) - UNOBSERVED * jnp.dot(slab_rows, item_gram, preferred_element_type=jnp.float32) - REGULAR * slab_rows.astype(jnp.float32)
        return newton(slab_rows, gradient, user_inverse)

    slabs = user_factors.reshape(N_USERS, USR_DEV, RANK)
    user_new = lax.map(user_slab, (slabs, coords, rating_tiles, tile_count))

    def item_slab(totals, packed):
        slab_rows, slab_coords, slab_ratings, slab_count = packed
        live_mask = (slot_ids < slab_count).astype(jnp.float32)[:, None, None]
        user_tiles = tile_rows(slab_rows, slab_coords[:, 0])
        item_tiles = tile_rows(item_factors, slab_coords[:, 1])
        errors_new = (live_mask * (slab_ratings.astype(jnp.float32) - predict(user_tiles, item_tiles))).astype(jnp.bfloat16)
        additions = jnp.einsum("sij,sik->sjk", errors_new.astype(jnp.float32), user_tiles.astype(jnp.float32))
        return totals.at[slab_coords[:, 1]].add(additions), None

    start = jnp.zeros((ITEMS // TILE, TILE, RANK), jnp.float32)
    observed, unused = lax.scan(item_slab, start, (user_new, coords, rating_tiles, tile_count))
    gradient = observed.reshape(ITEMS, RANK) - UNOBSERVED * jnp.dot(item_factors, user_gram, preferred_element_type=jnp.float32) - REGULAR * item_factors.astype(jnp.float32)
    item_new = newton(item_factors, gradient, item_inverse)
    return user_new.reshape(USERS, RANK), item_new
```

```python
import functools

import jax
import jax.numpy as jnp
from jax import lax
from jax.experimental import pallas as pl
from jax.experimental.pallas import tpu as pltpu
from jax.sharding import PartitionSpec as P

UNOBSERVED = 256.0
REGULAR = 2.0
HIGHEST = lax.Precision.HIGHEST
MESH = pl.DeviceIdType.MESH
NY = 4
PARTS = 4
SEMS = 144


class Net:
    def __init__(self, send_sem, recv_sem):
        self.send_sem = send_sem
        self.recv_sem = recv_sem
        self.used = 0
        self.started = []

    def slot(self):
        self.used += 1
        return self.used - 1

    def push(self, index, source, target, device):
        copy = pltpu.make_async_remote_copy(
            src_ref=source,
            dst_ref=target,
            send_sem=self.send_sem.at[index],
            recv_sem=self.recv_sem.at[index],
            device_id=device,
            device_id_type=MESH,
        )
        copy.start()
        self.started.append(copy)

    def land(self, index, target, device):
        pltpu.make_async_remote_copy(
            src_ref=target,
            dst_ref=target,
            send_sem=self.send_sem.at[index],
            recv_sem=self.recv_sem.at[index],
            device_id=device,
            device_id_type=MESH,
        ).wait_recv()

    def drain(self):
        for copy in self.started:
            copy.wait_send()
        self.started = []


class Ring:
    def __init__(self, net, size, place, to, piece):
        self.net, self.size, self.place, self.to, self.piece = net, size, place, to, piece
        self.slots = {}
        for distance in range(1, size // 2 + 1):
            self.slots[distance] = (net.slot(), net.slot())

    def steps(self):
        return self.size // 2

    def halves(self, distance):
        return (0, 1) if 2 * distance == self.size else (None, None)

    def send(self, distance):
        if distance > self.steps():
            return
        for index, step, half in zip(self.slots[distance], (1, -1), self.halves(distance)):
            chunk = lax.rem(self.place - step * (distance - 1) + self.size, self.size)
            view = self.piece(chunk, half)
            self.net.push(index, view, view, self.to(step))

    def recv(self, distance):
        if distance > self.steps():
            return []
        came = []
        for index, step, half in zip(self.slots[distance], (1, -1), self.halves(distance)):
            chunk = lax.rem(self.place - step * distance + self.size, self.size)
            self.net.land(index, self.piece(chunk, half), self.to(step))
            came.append((chunk, half))
        return came


class Sibling:
    def __init__(self, net, core, device):
        self.net, self.core, self.device = net, core, device
        self.due = []

    def hand(self, piece):
        index = self.net.slot()
        view = piece(self.core)
        self.net.push(index, view, view, self.device)
        self.due.append((index, piece))

    def collect(self):
        for index, piece in self.due:
            self.net.land(index, piece(1 - self.core), self.device)
        self.due = []


def kernel(
    nx, nz, meta, u_hbm, i_hbm, r_hbm, ig, ug, ui, ii, unew_out, inew_out,
    users, items, news, ratings, errors, sums, running, coupled, icoupled,
    qs, ra, sa, ta, rb, sb, tb, send_sem, recv_sem, local_sem,
):
    ny = NY
    u = lax.axis_index("users")
    c = lax.axis_index("dims")
    y, z = lax.div(u, nz), lax.rem(u, nz)
    x, k = lax.div(c, 2), lax.rem(c, 2)

    def device(xx, kk, yy, zz):
        return (yy * nz + zz, xx * 2 + kk)

    def along_x(step):
        return device(lax.rem(x + step + nx, nx), k, y, z)

    def along_y(step):
        return device(x, k, lax.rem(y + step + ny, ny), z)

    def along_z(step):
        return device(x, k, y, lax.rem(z + step + nz, nz))

    other_core = device(x, 1 - k, y, z)
    row_tiles, tile, width = users.shape[2:]
    slots = ratings.shape[0]
    panels = ny * nz // 2

    own = [
        pltpu.make_async_copy(i_hbm, items.at[k, x, y, z], local_sem.at[0]),
        pltpu.make_async_copy(u_hbm, users.at[k, x], local_sem.at[1]),
        pltpu.make_async_copy(r_hbm, ratings, local_sem.at[2]),
    ]
    for copy in own:
        copy.start()

    barrier = pltpu.get_barrier_semaphore()
    peers = [along_x(s) for s in range(1, nx)]
    peers += [along_y(s) for s in range(1, ny)]
    peers += [along_z(s) for s in range(1, nz)]
    peers += [other_core]
    for peer in peers:
        pl.semaphore_signal(barrier, inc=1, device_id=peer, device_id_type=MESH)
    pl.semaphore_wait(barrier, len(peers))

    net = Net(send_sem, recv_sem)
    sibling = Sibling(net, k, other_core)
    own[0].wait()
    own[1].wait()

    first = [net.slot() for _ in range(1, nx)]
    for index, step in zip(first, range(1, nx)):
        view = items.at[k, x, y, z]
        net.push(index, view, view, along_x(step))

    half_rows = row_tiles // 2

    def user_piece(table):
        def piece(chunk, half, kk=None):
            kk = k if kk is None else kk
            if half is None:
                return table.at[kk, chunk]
            return table.at[kk, chunk, pl.ds(half * half_rows, half_rows)]

        return piece

    xu = Ring(net, nx, x, along_x, user_piece(users))
    xu.send(1)
    sibling.hand(lambda kk: users.at[kk, x])
    for index, step in zip(first, range(1, nx)):
        source = lax.rem(x - step + nx, nx)
        net.land(index, items.at[k, source, y, z], along_x(step))

    hx = nx // 2

    def span(part, half):
        if half is None or hx < 2:
            return pl.ds(part * hx, hx)
        return pl.ds(part * hx + half * (hx // 2), hx // 2)

    def rows_of(half):
        size = items.shape[4]
        if half is None or hx >= 2:
            return pl.ds(0, size)
        return pl.ds(half * (size // 2), size // 2)

    ay = Ring(net, ny, y, along_y, lambda n, h, kk=None: items.at[k if kk is None else kk, span(0, h), n, z, rows_of(h)])
    bz = Ring(net, nz, z, along_z, lambda n, h, kk=None: items.at[k if kk is None else kk, span(1, h), y, n, rows_of(h)])
    az = Ring(net, nz, z, along_z, lambda n, h, kk=None: items.at[k if kk is None else kk, span(0, h), :, n, rows_of(h)])
    by = Ring(net, ny, y, along_y, lambda n, h, kk=None: items.at[k if kk is None else kk, span(1, h), n, :, rows_of(h)])

    def pass_on(ring, came):
        for chunk, half in came:
            sibling.hand(functools.partial(lambda kk, r, n, h: r.piece(n, h, kk), r=ring, n=chunk, h=half))

    ay.send(1)
    bz.send(1)
    for step in range(1, max(ay.steps(), bz.steps()) + 1):
        ay.recv(step)
        ay.send(step + 1)
        if step == ay.steps():
            az.send(1)
            sibling.hand(lambda kk: items.at[kk, span(0, None), :, z])
        bz.recv(step)
        bz.send(step + 1)
    if ay.steps() == 0:
        az.send(1)
        sibling.hand(lambda kk: items.at[kk, span(0, None), :, z])
    by.send(1)
    sibling.hand(lambda kk: items.at[kk, span(1, None), y, :])
    xu_step = 1
    for step in range(1, max(az.steps(), by.steps()) + 1):
        came = az.recv(step)
        az.send(step + 1)
        pass_on(az, came)
        if step >= 2 or az.steps() < 2:
            came = xu.recv(xu_step)
            xu.send(xu_step + 1)
            pass_on(xu, came)
            xu_step += 1
            came = by.recv(step - 1 if az.steps() >= 2 else step)
            by.send(step if az.steps() >= 2 else step + 1)
            pass_on(by, came)
    while xu_step <= xu.steps():
        pass_on(xu, xu.recv(xu_step))
        xu.send(xu_step + 1)
        xu_step += 1
    for step in range(max(az.steps(), 1), by.steps() + 1):
        if az.steps() >= 2:
            pass_on(by, by.recv(step))
    sibling.collect()
    own[2].wait()

    def whole_rank(table, row):
        return jnp.concatenate([table[kk, xx, row] for xx in range(nx) for kk in range(2)], axis=1)

    def panel_block(kk, xx, py, pz):
        return items[kk, xx, py, pl.ds(pz, 2)].reshape(tile, width)

    def error_tile(table, i):
        row, py, pz = meta[1, i], meta[2, i], meta[3, i]
        panel = jnp.concatenate([panel_block(kk, xx, py, pz) for xx in range(nx) for kk in range(2)], axis=1)
        prediction = lax.dot_general(
            whole_rank(table, row), panel, (((1,), (1,)), ((), ())), preferred_element_type=jnp.float32
        )
        live = meta[4, i].astype(jnp.float32)
        return (live * (ratings[meta[0, i]].astype(jnp.float32) - prediction)).astype(jnp.bfloat16)

    @pl.loop(0, row_tiles)
    def _(r):
        coupled[r] = jnp.dot(whole_rank(users, r), ig[...], preferred_element_type=jnp.float32)

    mine = jnp.concatenate([items[kk, xx, y, z] for xx in range(nx) for kk in range(2)], axis=1)
    icoupled[...] = jnp.dot(mine, ug[...], preferred_element_type=jnp.float32)

    running[...] = jnp.zeros_like(running)

    @pl.loop(0, slots)
    def _(i):
        error = error_tile(users, i)
        added = jnp.dot(error, panel_block(k, x, meta[2, i], meta[3, i]), preferred_element_type=jnp.float32)
        total = running[...] * meta[5, i].astype(jnp.float32) + added
        running[...] = total
        sums[i] = total

    def newton(factors, gradient, inverse):
        update = jnp.dot(gradient, inverse, precision=HIGHEST, preferred_element_type=jnp.float32)
        return (factors + update).astype(jnp.bfloat16)

    per = row_tiles // PARTS
    rings = []
    out_copies = []
    for part in range(PARTS):

        @pl.loop(part * per, (part + 1) * per)
        def _(r):
            observed = sums[meta[9, r]] * meta[10, r].astype(jnp.float32)
            factors = users[k, x, r].astype(jnp.float32)
            gradient = observed - UNOBSERVED * coupled[r] - REGULAR * factors
            news[k, x, r] = newton(factors, gradient, ui[...])

        def piece(chunk, half, kk=None, part=part):
            kk = k if kk is None else kk
            if half is None:
                return news.at[kk, chunk, pl.ds(part * per, per)]
            return news.at[kk, chunk, pl.ds(part * per, per), pl.ds(half * (tile // 2), tile // 2)]

        ring = Ring(net, nx, x, along_x, piece)
        ring.send(1)
        sibling.hand(functools.partial(lambda kk, f: f(x, None, kk), f=piece))
        rings.append(ring)
        copy = pltpu.make_async_copy(
            news.at[k, x, pl.ds(part * per, per)], unew_out.at[pl.ds(part * per, per)], local_sem.at[3 + part]
        )
        copy.start()
        out_copies.append(copy)
    for step in range(1, nx // 2 + 1):
        for ring in rings:
            came = ring.recv(step)
            ring.send(step + 1)
            pass_on(ring, came)
    sibling.collect()

    @pl.loop(0, slots)
    def _(i):
        errors[i] = error_tile(news, i)

    running[...] = jnp.zeros_like(running)

    @pl.loop(0, slots)
    def _(i):
        added = lax.dot_general(
            errors[meta[6, i]],
            news[k, x, meta[7, i]],
            (((0,), (0,)), ((), ())),
            preferred_element_type=jnp.float32,
        )
        total = running[...] * meta[8, i].astype(jnp.float32) + added
        running[...] = total
        sums[i] = total

    owner_rows = items.shape[4]

    @pl.loop(0, panels)
    def _(p):
        panel = sums[meta[11, p]] * meta[12, p].astype(jnp.float32)
        pair = panel.astype(jnp.bfloat16).reshape(2, owner_rows, width)
        qs[lax.div(p, nz // 2), pl.ds(2 * lax.rem(p, nz // 2), 2)] = pair

    na = ra.shape[2]
    a_rows, b_rows = pl.ds(0, na), pl.ds(na, owner_rows - na)
    b_slots = [net.slot() for _ in range(1, ny)]
    a_slots = [net.slot() for _ in range(1, nz)]
    for step in range(1, ny):
        to = lax.rem(y + step, ny)
        net.push(b_slots[step - 1], qs.at[to, :, b_rows], rb.at[step - 1], along_y(step))
    for step in range(1, nz):
        to = lax.rem(z + step, nz)
        net.push(a_slots[step - 1], qs.at[:, to, a_rows], ra.at[step - 1], along_z(step))
    for step in range(1, nz):
        net.land(a_slots[step - 1], ra.at[step - 1], along_z(step))
    total = qs[:, z, a_rows].astype(jnp.float32)
    for step in range(1, nz):
        total = total + ra[step - 1].astype(jnp.float32)
    sa[...] = total.astype(jnp.bfloat16)
    c_slots = [net.slot() for _ in range(1, ny)]
    for step in range(1, ny):
        to = lax.rem(y + step, ny)
        net.push(c_slots[step - 1], sa.at[to], ta.at[step - 1], along_y(step))
    for step in range(1, ny):
        net.land(b_slots[step - 1], rb.at[step - 1], along_y(step))
    total = qs[y, :, b_rows].astype(jnp.float32)
    for step in range(1, ny):
        total = total + rb[step - 1].astype(jnp.float32)
    sb[...] = total.astype(jnp.bfloat16)
    d_slots = [net.slot() for _ in range(1, nz)]
    for step in range(1, nz):
        to = lax.rem(z + step, nz)
        net.push(d_slots[step - 1], sb.at[to], tb.at[step - 1], along_z(step))
    for step in range(1, ny):
        net.land(c_slots[step - 1], ta.at[step - 1], along_y(step))
    total_a = sa[y].astype(jnp.float32)
    for step in range(1, ny):
        total_a = total_a + ta[step - 1].astype(jnp.float32)
    for step in range(1, nz):
        net.land(d_slots[step - 1], tb.at[step - 1], along_z(step))
    total_b = sb[z].astype(jnp.float32)
    for step in range(1, nz):
        total_b = total_b + tb[step - 1].astype(jnp.float32)
    observed = jnp.concatenate([total_a, total_b], axis=0)
    factors = items[k, x, y, z].astype(jnp.float32)
    gradient = observed - UNOBSERVED * icoupled[...] - REGULAR * factors
    inew_out[...] = newton(factors, gradient, ii[...])
    for copy in out_copies:
        copy.wait()
    net.drain()


def lookup(tile_coords, tile_count, row_tiles, panel_count, nz):
    count = tile_coords.shape[0]
    row, panel = tile_coords[:, 0], tile_coords[:, 1]
    slot = lax.iota(jnp.int32, count)
    live = (slot < tile_count[0]).astype(jnp.int32)

    def rank_of(value):
        key = value * count + slot
        return jnp.sum((key[None, :] < key[:, None]).astype(jnp.int32), axis=1)

    def sort_by(rank, value):
        return jnp.sum(jnp.where(rank[None, :] == slot[:, None], value[None, :], 0), axis=1)

    def same(value):
        return jnp.concatenate([jnp.zeros((1,), jnp.int32), (value[1:] == value[:-1]).astype(jnp.int32)])

    def last(value, size):
        ids = lax.iota(jnp.int32, size)[:, None]
        upto = jnp.sum((value[None, :] <= ids).astype(jnp.int32), axis=1)
        has = jnp.any(value[None, :] == ids, axis=1).astype(jnp.int32)
        return jnp.maximum(upto - 1, 0), has

    by_row, by_panel = rank_of(row), rank_of(panel)
    sorted_row, sorted_panel = sort_by(by_row, row), sort_by(by_row, panel)
    last_row, has_row = last(row, row_tiles)
    last_panel, has_panel = last(panel, panel_count)
    lines = [
        sort_by(by_row, slot),
        sorted_row,
        sorted_panel // (nz // 2),
        2 * (sorted_panel % (nz // 2)),
        sort_by(by_row, live),
        same(sorted_row),
        sort_by(by_panel, by_row),
        sort_by(by_panel, row),
        same(sort_by(by_panel, panel)),
        last_row,
        has_row,
        last_panel,
        has_panel,
    ]
    wide = max(count, row_tiles, panel_count)
    return jnp.stack([jnp.pad(line, (0, wide - line.shape[0])) for line in lines])


def local(nx, nz, user_factors, item_factors, ratings, tile_coords, tile_count, item_gram, user_gram, user_inverse, item_inverse):
    user_rows, width = user_factors.shape
    owner_rows = item_factors.shape[0]
    slots, tile, _ = ratings.shape
    row_tiles = user_rows // tile
    panel_count = NY * nz * owner_rows // tile
    meta = lookup(tile_coords, tile_count, row_tiles, panel_count, nz)
    na = owner_rows // 4
    nb = owner_rows - na
    bf16, f32 = jnp.bfloat16, jnp.float32
    vmem = pl.BlockSpec(memory_space=pltpu.VMEM)
    hbm = pl.BlockSpec(memory_space=pl.ANY)
    user_new, item_new = pl.pallas_call(
        functools.partial(kernel, nx, nz),
        out_shape=(
            jax.ShapeDtypeStruct((row_tiles, tile, width), bf16),
            jax.ShapeDtypeStruct((owner_rows, width), bf16),
        ),
        in_specs=[pl.BlockSpec(memory_space=pltpu.SMEM), hbm, hbm, hbm, vmem, vmem, vmem, vmem],
        out_specs=(hbm, vmem),
        scratch_shapes=[
            pltpu.VMEM((2, nx, row_tiles, tile, width), bf16),
            pltpu.VMEM((2, nx, NY, nz, owner_rows, width), bf16),
            pltpu.VMEM((2, nx, row_tiles, tile, width), bf16),
            pltpu.VMEM((slots, tile, tile), bf16),
            pltpu.VMEM((slots, tile, tile), bf16),
            pltpu.VMEM((slots, tile, width), f32),
            pltpu.VMEM((tile, width), f32),
            pltpu.VMEM((row_tiles, tile, width), f32),
            pltpu.VMEM((owner_rows, width), f32),
            pltpu.VMEM((NY, nz, owner_rows, width), bf16),
            pltpu.VMEM((nz - 1, NY, na, width), bf16),
            pltpu.VMEM((NY, na, width), bf16),
            pltpu.VMEM((max(NY - 1, 1), na, width), bf16),
            pltpu.VMEM((max(NY - 1, 1), nz, nb, width), bf16),
            pltpu.VMEM((nz, nb, width), bf16),
            pltpu.VMEM((nz - 1, nb, width), bf16),
            pltpu.SemaphoreType.DMA((SEMS,)),
            pltpu.SemaphoreType.DMA((SEMS,)),
            pltpu.SemaphoreType.DMA((3 + PARTS,)),
        ],
        compiler_params=pltpu.CompilerParams(
            collective_id=0, has_side_effects=True, vmem_limit_bytes=56 * 1024 * 1024
        ),
    )(
        meta,
        user_factors.reshape(row_tiles, tile, width),
        item_factors,
        ratings,
        item_gram,
        user_gram,
        user_inverse,
        item_inverse,
    )
    return user_new.reshape(user_rows, width), item_new


def solution(mesh):
    placed = (
        P("users", "dims"),
        P("users", "dims"),
        P("users", None, None),
        P("users", None),
        P("users"),
        P(None, "dims"),
        P(None, "dims"),
        P("dims", None),
        P("dims", None),
    )
    return jax.shard_map(
        functools.partial(local, mesh.shape["dims"] // 2, mesh.shape["users"] // NY),
        mesh=mesh,
        in_specs=placed,
        out_specs=(P("users", "dims"), P("users", "dims")),
        check_vma=False,
    )
```

```python
import functools

import jax
import jax.numpy as jnp
from jax import lax
from jax.experimental import pallas as pl
from jax.experimental.pallas import tpu as pltpu
from jax.sharding import PartitionSpec as P

UNOBSERVED = 256.0
REGULAR = 2.0
HIGHEST = lax.Precision.HIGHEST
MESH = pl.DeviceIdType.MESH
NY = 4
PARTS = 4
SEMS = 240
UNROLL = 5


class Net:
    def __init__(self, send_sem, recv_sem):
        self.send_sem = send_sem
        self.recv_sem = recv_sem
        self.used = 0
        self.started = []

    def slot(self):
        self.used += 1
        return self.used - 1

    def push(self, index, source, target, device):
        copy = pltpu.make_async_remote_copy(
            src_ref=source,
            dst_ref=target,
            send_sem=self.send_sem.at[index],
            recv_sem=self.recv_sem.at[index],
            device_id=device,
            device_id_type=MESH,
        )
        copy.start()
        self.started.append(copy)

    def land(self, index, target, device):
        pltpu.make_async_remote_copy(
            src_ref=target,
            dst_ref=target,
            send_sem=self.send_sem.at[index],
            recv_sem=self.recv_sem.at[index],
            device_id=device,
            device_id_type=MESH,
        ).wait_recv()

    def drain(self):
        for copy in self.started:
            copy.wait_send()
        self.started = []


class Ring:
    def __init__(self, net, size, place, to, piece):
        self.net, self.size, self.place, self.to, self.piece = net, size, place, to, piece
        self.slots = {}
        for distance in range(1, size // 2 + 1):
            self.slots[distance] = (net.slot(), net.slot())

    def steps(self):
        return self.size // 2

    def halves(self, distance):
        return (0, 1) if 2 * distance == self.size else (None, None)

    def send(self, distance):
        if distance > self.steps():
            return
        for index, step, half in zip(self.slots[distance], (1, -1), self.halves(distance)):
            chunk = lax.rem(self.place - step * (distance - 1) + self.size, self.size)
            view = self.piece(chunk, half)
            self.net.push(index, view, view, self.to(step))

    def recv(self, distance):
        if distance > self.steps():
            return []
        came = []
        for index, step, half in zip(self.slots[distance], (1, -1), self.halves(distance)):
            chunk = lax.rem(self.place - step * distance + self.size, self.size)
            self.net.land(index, self.piece(chunk, half), self.to(step))
            came.append((chunk, half))
        return came


class Sibling:
    def __init__(self, net, core, device):
        self.net, self.core, self.device = net, core, device
        self.due = {}

    def hand(self, piece):
        index = self.net.slot()
        view = piece(self.core)
        self.net.push(index, view, view, self.device)
        self.due[index] = piece
        return index

    def wait(self, index):
        self.net.land(index, self.due.pop(index)(1 - self.core), self.device)

    def collect(self):
        for index in list(self.due):
            self.wait(index)


def kernel(
    nx, nz, meta, u_hbm, i_hbm, r_hbm, ig, ug, ui, ii, unew_out, inew_out,
    users, items, news, ratings, errors, sums, running, coupled, icoupled,
    qs, ra, sa, ta, rb, sb, tb, send_sem, recv_sem, local_sem,
):
    ny = NY
    u = lax.axis_index("users")
    c = lax.axis_index("dims")
    y, z = lax.div(u, nz), lax.rem(u, nz)
    x, k = lax.div(c, 2), lax.rem(c, 2)

    def device(xx, kk, yy, zz):
        return (yy * nz + zz, xx * 2 + kk)

    def along_x(step):
        return device(lax.rem(x + step + nx, nx), k, y, z)

    def along_y(step):
        return device(x, k, lax.rem(y + step + ny, ny), z)

    def along_z(step):
        return device(x, k, y, lax.rem(z + step + nz, nz))

    other_core = device(x, 1 - k, y, z)
    row_tiles, tile, width = users.shape[2:]
    slots = ratings.shape[0]
    panels = ny * nz // 2

    own = [
        pltpu.make_async_copy(i_hbm, items.at[k, x, y, z], local_sem.at[0]),
        pltpu.make_async_copy(u_hbm, users.at[k, x], local_sem.at[1]),
        pltpu.make_async_copy(r_hbm, ratings, local_sem.at[2]),
    ]
    for copy in own:
        copy.start()

    barrier = pltpu.get_barrier_semaphore()
    peers = [along_x(s) for s in range(1, nx)]
    peers += [along_y(s) for s in range(1, ny)]
    peers += [along_z(s) for s in range(1, nz)]
    peers += [other_core]
    for peer in peers:
        pl.semaphore_signal(barrier, inc=1, device_id=peer, device_id_type=MESH)
    pl.semaphore_wait(barrier, len(peers))

    net = Net(send_sem, recv_sem)
    sibling = Sibling(net, k, other_core)
    own[0].wait()
    own[1].wait()

    first = [net.slot() for _ in range(1, nx)]
    for index, step in zip(first, range(1, nx)):
        view = items.at[k, x, y, z]
        net.push(index, view, view, along_x(step))

    half_rows = row_tiles // 2

    def user_piece(table):
        def piece(chunk, half, kk=None):
            kk = k if kk is None else kk
            if half is None:
                return table.at[kk, chunk]
            return table.at[kk, chunk, pl.ds(half * half_rows, half_rows)]

        return piece

    xu = Ring(net, nx, x, along_x, user_piece(users))
    xu.send(1)
    own_users = sibling.hand(lambda kk: users.at[kk, x])
    for index, step in zip(first, range(1, nx)):
        source = lax.rem(x - step + nx, nx)
        net.land(index, items.at[k, source, y, z], along_x(step))

    hx = nx // 2

    def span(part, half):
        if half is None or hx < 2:
            return pl.ds(part * hx, hx)
        return pl.ds(part * hx + half * (hx // 2), hx // 2)

    def rows_of(half):
        size = items.shape[4]
        if half is None or hx >= 2:
            return pl.ds(0, size)
        return pl.ds(half * (size // 2), size // 2)

    def pass_on(ring, came):
        return [sibling.hand(functools.partial(ring.piece, chunk, half)) for chunk, half in came]

    active = []

    def start(ring, arrived):
        ring.send(1)
        active.append([ring, 1, arrived])

    def wave():
        for entry in list(active):
            ring, step, arrived = entry
            if step <= ring.steps():
                came = ring.recv(step)
                ring.send(step + 1)
                arrived(step, came)
                entry[1] += 1

    def second_z(yy, is_last):
        def arrived(step, came):
            for n, h in came if is_last else []:
                sibling.hand(lambda kk, n=n, h=h: items.at[kk, span(0, h), :, n, rows_of(h)])

        start(Ring(net, nz, z, along_z, lambda n, h, kk=None: items.at[k if kk is None else kk, span(0, h), yy, n, rows_of(h)]), arrived)

    def second_y(zz, is_last):
        def arrived(step, came):
            for n, h in came if is_last else []:
                sibling.hand(lambda kk, n=n, h=h: items.at[kk, span(1, h), n, :, rows_of(h)])

        start(Ring(net, ny, y, along_y, lambda n, h, kk=None: items.at[k if kk is None else kk, span(1, h), n, zz, rows_of(h)]), arrived)

    def first_y(step, came):
        at_end = step == ay.steps()
        for chunk in [came[0][0]] if at_end else [n for n, _ in came]:
            second_z(chunk, at_end)
        if at_end:
            sibling.hand(lambda kk: items.at[kk, span(0, None), :, z])

    def first_z(step, came):
        at_end = step == bz.steps()
        for chunk in [came[0][0]] if at_end else [n for n, _ in came]:
            second_y(chunk, at_end)
        if at_end:
            sibling.hand(lambda kk: items.at[kk, span(1, None), y, :])

    def couple(chunk, begin):
        @pl.loop(0, row_tiles)
        def _(r):
            pair = jnp.concatenate([users[0, chunk, r], users[1, chunk, r]], axis=1)
            product = jnp.dot(pair, ig[chunk], preferred_element_type=jnp.float32)
            coupled[r] = product if begin else coupled[r] + product

    ay = Ring(net, ny, y, along_y, lambda n, h, kk=None: items.at[k if kk is None else kk, span(0, h), n, z, rows_of(h)])
    bz = Ring(net, nz, z, along_z, lambda n, h, kk=None: items.at[k if kk is None else kk, span(1, h), y, n, rows_of(h)])
    start(ay, first_y)
    start(bz, first_z)
    second_z(y, ay.steps() == 0)
    second_y(z, bz.steps() == 0)
    if ay.steps() == 0:
        sibling.hand(lambda kk: items.at[kk, span(0, None), :, z])
    waves = ay.steps() + nz // 2
    waves = max(waves, bz.steps() + ny // 2)
    user_hands = []
    met = xu_step = 0
    for number in range(1, waves + 1):
        wave()
        if number == 2 or (number == waves and number < 2):
            sibling.wait(own_users)
            couple(x, True)
        if number in (3, 5) and xu_step < xu.steps():
            xu_step += 1
            came = xu.recv(xu_step)
            xu.send(xu_step + 1)
            user_hands.append((came, pass_on(xu, came)))
        if number == 4 and user_hands and 2 < nx:
            came, hands = user_hands[0]
            for (chunk, _), hand in zip(came, hands):
                sibling.wait(hand)
                couple(chunk, False)
            met = 1
    while xu_step < xu.steps():
        xu_step += 1
        came = xu.recv(xu_step)
        xu.send(xu_step + 1)
        user_hands.append((came, pass_on(xu, came)))
    for step, (came, hands) in enumerate(user_hands):
        if step >= met:
            for hand in hands:
                sibling.wait(hand)
            for chunk in [came[0][0]] if step == xu.steps() - 1 else [n for n, _ in came]:
                couple(chunk, False)
    sibling.collect()
    own[2].wait()

    def whole_rank(table, row):
        return jnp.concatenate([table[kk, xx, row] for xx in range(nx) for kk in range(2)], axis=1)

    def panel_block(kk, xx, py, pz):
        return items[kk, xx, py, pl.ds(pz, 2)].reshape(tile, width)

    def error_tile(table, i):
        row, py, pz = meta[1, i], meta[2, i], meta[3, i]
        panel = jnp.concatenate([panel_block(kk, xx, py, pz) for xx in range(nx) for kk in range(2)], axis=1)
        prediction = lax.dot_general(
            whole_rank(table, row), panel, (((1,), (1,)), ((), ())), preferred_element_type=jnp.float32
        )
        live = meta[4, i].astype(jnp.float32)
        return (live * (ratings[meta[0, i]].astype(jnp.float32) - prediction)).astype(jnp.bfloat16)

    running[...] = jnp.zeros_like(running)

    @pl.loop(0, slots, unroll=UNROLL)
    def _(i):
        error = error_tile(users, i)
        added = jnp.dot(error, panel_block(k, x, meta[2, i], meta[3, i]), preferred_element_type=jnp.float32)
        total = running[...] * meta[5, i].astype(jnp.float32) + added
        running[...] = total
        sums[i] = total

    def newton(factors, gradient, inverse):
        update = jnp.dot(gradient, inverse, precision=HIGHEST, preferred_element_type=jnp.float32)
        return (factors + update).astype(jnp.bfloat16)

    per = row_tiles // PARTS
    rings = []
    out_copies = []
    for part in range(PARTS):

        @pl.loop(part * per, (part + 1) * per)
        def _(r):
            observed = sums[meta[9, r]] * meta[10, r].astype(jnp.float32)
            factors = users[k, x, r].astype(jnp.float32)
            gradient = observed - UNOBSERVED * coupled[r] - REGULAR * factors
            news[k, x, r] = newton(factors, gradient, ui[...])

        def piece(chunk, half, kk=None, part=part):
            kk = k if kk is None else kk
            if half is None:
                return news.at[kk, chunk, pl.ds(part * per, per)]
            return news.at[kk, chunk, pl.ds(part * per, per), pl.ds(half * (tile // 2), tile // 2)]

        ring = Ring(net, nx, x, along_x, piece)
        ring.send(1)
        sibling.hand(functools.partial(piece, x, None))
        rings.append(ring)
        copy = pltpu.make_async_copy(
            news.at[k, x, pl.ds(part * per, per)], unew_out.at[pl.ds(part * per, per)], local_sem.at[3 + part]
        )
        copy.start()
        out_copies.append(copy)
    mine = jnp.concatenate([items[kk, xx, y, z] for xx in range(nx) for kk in range(2)], axis=1)
    icoupled[...] = jnp.dot(mine, ug[...], preferred_element_type=jnp.float32)

    for step in range(1, nx // 2 + 1):
        for ring in rings:
            came = ring.recv(step)
            ring.send(step + 1)
            pass_on(ring, came)
    sibling.collect()

    @pl.loop(0, slots, unroll=UNROLL)
    def _(i):
        errors[i] = error_tile(news, i)

    running[...] = jnp.zeros_like(running)

    @pl.loop(0, slots, unroll=UNROLL)
    def _(i):
        added = lax.dot_general(
            errors[meta[6, i]],
            news[k, x, meta[7, i]],
            (((0,), (0,)), ((), ())),
            preferred_element_type=jnp.float32,
        )
        total = running[...] * meta[8, i].astype(jnp.float32) + added
        running[...] = total
        sums[i] = total

    owner_rows = items.shape[4]

    @pl.loop(0, panels)
    def _(p):
        panel = sums[meta[11, p]] * meta[12, p].astype(jnp.float32)
        pair = panel.astype(jnp.bfloat16).reshape(2, owner_rows, width)
        qs[lax.div(p, nz // 2), pl.ds(2 * lax.rem(p, nz // 2), 2)] = pair

    na = ra.shape[2]
    a_rows, b_rows = pl.ds(0, na), pl.ds(na, owner_rows - na)
    b_slots = [net.slot() for _ in range(1, ny)]
    a_slots = [net.slot() for _ in range(1, nz)]
    for step in range(1, ny):
        to = lax.rem(y + step, ny)
        net.push(b_slots[step - 1], qs.at[to, :, b_rows], rb.at[step - 1], along_y(step))
    for step in range(1, nz):
        to = lax.rem(z + step, nz)
        net.push(a_slots[step - 1], qs.at[:, to, a_rows], ra.at[step - 1], along_z(step))
    for step in range(1, nz):
        net.land(a_slots[step - 1], ra.at[step - 1], along_z(step))
    total = qs[:, z, a_rows].astype(jnp.float32)
    for step in range(1, nz):
        total = total + ra[step - 1].astype(jnp.float32)
    sa[...] = total.astype(jnp.bfloat16)
    c_slots = [net.slot() for _ in range(1, ny)]
    for step in range(1, ny):
        to = lax.rem(y + step, ny)
        net.push(c_slots[step - 1], sa.at[to], ta.at[step - 1], along_y(step))
    for step in range(1, ny):
        net.land(b_slots[step - 1], rb.at[step - 1], along_y(step))
    total = qs[y, :, b_rows].astype(jnp.float32)
    for step in range(1, ny):
        total = total + rb[step - 1].astype(jnp.float32)
    sb[...] = total.astype(jnp.bfloat16)
    d_slots = [net.slot() for _ in range(1, nz)]
    for step in range(1, nz):
        to = lax.rem(z + step, nz)
        net.push(d_slots[step - 1], sb.at[to], tb.at[step - 1], along_z(step))
    for step in range(1, ny):
        net.land(c_slots[step - 1], ta.at[step - 1], along_y(step))
    total_a = sa[y].astype(jnp.float32)
    for step in range(1, ny):
        total_a = total_a + ta[step - 1].astype(jnp.float32)
    for step in range(1, nz):
        net.land(d_slots[step - 1], tb.at[step - 1], along_z(step))
    total_b = sb[z].astype(jnp.float32)
    for step in range(1, nz):
        total_b = total_b + tb[step - 1].astype(jnp.float32)
    observed = jnp.concatenate([total_a, total_b], axis=0)
    factors = items[k, x, y, z].astype(jnp.float32)
    gradient = observed - UNOBSERVED * icoupled[...] - REGULAR * factors
    inew_out[...] = newton(factors, gradient, ii[...])
    for copy in out_copies:
        copy.wait()
    net.drain()


def lookup(tile_coords, tile_count, row_tiles, panel_count, nz):
    count = tile_coords.shape[0]
    row, panel = tile_coords[:, 0], tile_coords[:, 1]
    slot = lax.iota(jnp.int32, count)
    live = (slot < tile_count[0]).astype(jnp.int32)

    def rank_of(value):
        key = value * count + slot
        return jnp.sum((key[None, :] < key[:, None]).astype(jnp.int32), axis=1)

    def sort_by(rank, value):
        return jnp.sum(jnp.where(rank[None, :] == slot[:, None], value[None, :], 0), axis=1)

    def same(value):
        return jnp.concatenate([jnp.zeros((1,), jnp.int32), (value[1:] == value[:-1]).astype(jnp.int32)])

    def last(value, size):
        ids = lax.iota(jnp.int32, size)[:, None]
        upto = jnp.sum((value[None, :] <= ids).astype(jnp.int32), axis=1)
        has = jnp.any(value[None, :] == ids, axis=1).astype(jnp.int32)
        return jnp.maximum(upto - 1, 0), has

    by_row, by_panel = rank_of(row), rank_of(panel)
    sorted_row, sorted_panel = sort_by(by_row, row), sort_by(by_row, panel)
    last_row, has_row = last(row, row_tiles)
    last_panel, has_panel = last(panel, panel_count)
    lines = [
        sort_by(by_row, slot),
        sorted_row,
        sorted_panel // (nz // 2),
        2 * (sorted_panel % (nz // 2)),
        sort_by(by_row, live),
        same(sorted_row),
        sort_by(by_panel, by_row),
        sort_by(by_panel, row),
        same(sort_by(by_panel, panel)),
        last_row,
        has_row,
        last_panel,
        has_panel,
    ]
    wide = max(count, row_tiles, panel_count)
    return jnp.stack([jnp.pad(line, (0, wide - line.shape[0])) for line in lines])


def local(nx, nz, user_factors, item_factors, ratings, tile_coords, tile_count, item_gram, user_gram, user_inverse, item_inverse):
    user_rows, width = user_factors.shape
    owner_rows = item_factors.shape[0]
    slots, tile, _ = ratings.shape
    row_tiles = user_rows // tile
    panel_count = NY * nz * owner_rows // tile
    meta = lookup(tile_coords, tile_count, row_tiles, panel_count, nz)
    na = owner_rows // 4
    nb = owner_rows - na
    bf16, f32 = jnp.bfloat16, jnp.float32
    vmem = pl.BlockSpec(memory_space=pltpu.VMEM)
    hbm = pl.BlockSpec(memory_space=pl.ANY)
    user_new, item_new = pl.pallas_call(
        functools.partial(kernel, nx, nz),
        out_shape=(
            jax.ShapeDtypeStruct((row_tiles, tile, width), bf16),
            jax.ShapeDtypeStruct((owner_rows, width), bf16),
        ),
        in_specs=[pl.BlockSpec(memory_space=pltpu.SMEM), hbm, hbm, hbm, vmem, vmem, vmem, vmem],
        out_specs=(hbm, vmem),
        scratch_shapes=[
            pltpu.VMEM((2, nx, row_tiles, tile, width), bf16),
            pltpu.VMEM((2, nx, NY, nz, owner_rows, width), bf16),
            pltpu.VMEM((2, nx, row_tiles, tile, width), bf16),
            pltpu.VMEM((slots, tile, tile), bf16),
            pltpu.VMEM((slots, tile, tile), bf16),
            pltpu.VMEM((slots, tile, width), f32),
            pltpu.VMEM((tile, width), f32),
            pltpu.VMEM((row_tiles, tile, width), f32),
            pltpu.VMEM((owner_rows, width), f32),
            pltpu.VMEM((NY, nz, owner_rows, width), bf16),
            pltpu.VMEM((nz - 1, NY, na, width), bf16),
            pltpu.VMEM((NY, na, width), bf16),
            pltpu.VMEM((max(NY - 1, 1), na, width), bf16),
            pltpu.VMEM((max(NY - 1, 1), nz, nb, width), bf16),
            pltpu.VMEM((nz, nb, width), bf16),
            pltpu.VMEM((nz - 1, nb, width), bf16),
            pltpu.SemaphoreType.DMA((SEMS,)),
            pltpu.SemaphoreType.DMA((SEMS,)),
            pltpu.SemaphoreType.DMA((3 + PARTS,)),
        ],
        compiler_params=pltpu.CompilerParams(
            collective_id=0, has_side_effects=True, vmem_limit_bytes=56 * 1024 * 1024
        ),
    )(
        meta,
        user_factors.reshape(row_tiles, tile, width),
        item_factors,
        ratings,
        item_gram.reshape(nx, 2 * width, width),
        user_gram,
        user_inverse,
        item_inverse,
    )
    return user_new.reshape(user_rows, width), item_new


def solution(mesh):
    placed = (
        P("users", "dims"),
        P("users", "dims"),
        P("users", None, None),
        P("users", None),
        P("users"),
        P(None, "dims"),
        P(None, "dims"),
        P("dims", None),
        P("dims", None),
    )
    return jax.shard_map(
        functools.partial(local, mesh.shape["dims"] // 2, mesh.shape["users"] // NY),
        mesh=mesh,
        in_specs=placed,
        out_specs=(P("users", "dims"), P("users", "dims")),
        check_vma=False,
    )
```

```python
import functools

import jax
import jax.numpy as jnp
from jax import lax
from jax.experimental import pallas as pl
from jax.experimental.pallas import tpu as pltpu
from jax.sharding import PartitionSpec as P

UNOBSERVED = 256.0
REGULAR = 2.0
HIGHEST = lax.Precision.HIGHEST
MESH = pl.DeviceIdType.MESH
NY = 4
PARTS = 4
SEMS = 240
UNROLL = 5


class Net:
    def __init__(self, send_sem, recv_sem):
        self.send_sem = send_sem
        self.recv_sem = recv_sem
        self.used = 0
        self.started = []

    def slot(self):
        self.used += 1
        return self.used - 1

    def push(self, index, source, target, device):
        copy = pltpu.make_async_remote_copy(
            src_ref=source,
            dst_ref=target,
            send_sem=self.send_sem.at[index],
            recv_sem=self.recv_sem.at[index],
            device_id=device,
            device_id_type=MESH,
        )
        copy.start()
        self.started.append(copy)

    def land(self, index, target, device):
        pltpu.make_async_remote_copy(
            src_ref=target,
            dst_ref=target,
            send_sem=self.send_sem.at[index],
            recv_sem=self.recv_sem.at[index],
            device_id=device,
            device_id_type=MESH,
        ).wait_recv()

    def drain(self):
        for copy in self.started:
            copy.wait_send()
        self.started = []


class Ring:
    def __init__(self, net, size, place, to, piece):
        self.net, self.size, self.place, self.to, self.piece = net, size, place, to, piece
        self.slots = {}
        for distance in range(1, size // 2 + 1):
            self.slots[distance] = (net.slot(), net.slot())

    def steps(self):
        return self.size // 2

    def halves(self, distance):
        return (0, 1) if 2 * distance == self.size else (None, None)

    def send(self, distance):
        if distance > self.steps():
            return
        for index, step, half in zip(self.slots[distance], (1, -1), self.halves(distance)):
            chunk = lax.rem(self.place - step * (distance - 1) + self.size, self.size)
            view = self.piece(chunk, half)
            self.net.push(index, view, view, self.to(step))

    def recv(self, distance):
        if distance > self.steps():
            return []
        came = []
        for index, step, half in zip(self.slots[distance], (1, -1), self.halves(distance)):
            chunk = lax.rem(self.place - step * distance + self.size, self.size)
            self.net.land(index, self.piece(chunk, half), self.to(step))
            came.append((chunk, half))
        return came


class Direct:
    def __init__(self, net, size, place, to, piece):
        self.net, self.size, self.place, self.to, self.piece = net, size, place, to, piece
        near = [step for step in (1, -1, 2, -2) if abs(step) < size]
        near = [step for n, step in enumerate(near) if step % size not in [e % size for e in near[:n]]]
        self.plan = [[(net.slot(), 0, step, None) for step in near]] if near else []
        if size == 8:
            self.plan.append([(net.slot(), 2, 1, None), (net.slot(), -2, -1, None), (net.slot(), 2, 2, 0), (net.slot(), -2, -2, 1)])

    def steps(self):
        return len(self.plan)

    def chunk(self, back):
        return lax.rem(self.place - back + self.size, self.size)

    def send(self, step):
        if step > self.steps():
            return
        for index, back, jump, half in self.plan[step - 1]:
            view = self.piece(self.chunk(back), half)
            self.net.push(index, view, view, self.to(jump))

    def recv(self, step):
        came = []
        for index, back, jump, half in self.plan[step - 1]:
            chunk = self.chunk(back + jump)
            self.net.land(index, self.piece(chunk, half), self.to(jump))
            if half != 0:
                came.append(chunk)
        return came


class Sibling:
    def __init__(self, net, core, device):
        self.net, self.core, self.device = net, core, device
        self.due = {}

    def hand(self, piece):
        index = self.net.slot()
        view = piece(self.core)
        self.net.push(index, view, view, self.device)
        self.due[index] = piece
        return index

    def wait(self, index):
        self.net.land(index, self.due.pop(index)(1 - self.core), self.device)

    def collect(self):
        for index in list(self.due):
            self.wait(index)


def kernel(
    nx, nz, meta, u_hbm, i_hbm, r_hbm, ig, ug, ui, ii, unew_out, inew_out,
    users, items, news, ratings, errors, sums, running, coupled, icoupled,
    qs, ra, sa, ta, rb, sb, tb, send_sem, recv_sem, local_sem,
):
    ny = NY
    u = lax.axis_index("users")
    c = lax.axis_index("dims")
    y, z = lax.div(u, nz), lax.rem(u, nz)
    x, k = lax.div(c, 2), lax.rem(c, 2)

    def device(xx, kk, yy, zz):
        return (yy * nz + zz, xx * 2 + kk)

    def along_x(step):
        return device(lax.rem(x + step + nx, nx), k, y, z)

    def along_y(step):
        return device(x, k, lax.rem(y + step + ny, ny), z)

    def along_z(step):
        return device(x, k, y, lax.rem(z + step + nz, nz))

    other_core = device(x, 1 - k, y, z)
    row_tiles, tile, width = users.shape[2:]
    slots = ratings.shape[0]
    panels = ny * nz // 2

    own = [
        pltpu.make_async_copy(i_hbm, items.at[k, x, y, z], local_sem.at[0]),
        pltpu.make_async_copy(u_hbm, users.at[k, x], local_sem.at[1]),
        pltpu.make_async_copy(r_hbm, ratings, local_sem.at[2]),
    ]
    for copy in own:
        copy.start()

    barrier = pltpu.get_barrier_semaphore()
    peers = [along_x(s) for s in range(1, nx)]
    peers += [along_y(s) for s in range(1, ny)]
    peers += [along_z(s) for s in range(1, nz)]
    peers += [other_core]
    for peer in peers:
        pl.semaphore_signal(barrier, inc=1, device_id=peer, device_id_type=MESH)
    pl.semaphore_wait(barrier, len(peers))

    net = Net(send_sem, recv_sem)
    sibling = Sibling(net, k, other_core)
    own[0].wait()
    own[1].wait()

    first = [net.slot() for _ in range(1, nx)]
    for index, step in zip(first, range(1, nx)):
        view = items.at[k, x, y, z]
        net.push(index, view, view, along_x(step))

    half_rows = row_tiles // 2

    def user_piece(table):
        def piece(chunk, half, kk=None):
            kk = k if kk is None else kk
            if half is None:
                return table.at[kk, chunk]
            return table.at[kk, chunk, pl.ds(half * half_rows, half_rows)]

        return piece

    xu = Ring(net, nx, x, along_x, user_piece(users))
    xu.send(1)
    own_users = sibling.hand(lambda kk: users.at[kk, x])
    for index, step in zip(first, range(1, nx)):
        source = lax.rem(x - step + nx, nx)
        net.land(index, items.at[k, source, y, z], along_x(step))

    owner_rows = items.shape[4]
    split = owner_rows * 3 // 8 // 16 * 16

    def blocks(half):
        if half is None or nx < 2:
            return pl.ds(0, nx)
        return pl.ds(half * (nx // 2), nx // 2)

    def rows_of(part, half):
        low, size = (split, owner_rows - split) if part else (0, split)
        if half is None or nx >= 2:
            return pl.ds(low, size)
        return pl.ds(low + half * (size // 2), size // 2)

    def item_piece(part, yy, zz, half, kk=None):
        return items.at[k if kk is None else kk, blocks(half), yy, zz, rows_of(part, half)]

    def pass_on(ring, came):
        return [sibling.hand(functools.partial(ring.piece, chunk, half)) for chunk, half in came]

    active = []
    whole = slice(None)

    def start(order, ring, arrived):
        ring.send(1)
        active.append([order, ring, 1, arrived])

    def wave():
        for entry in sorted(active, key=lambda entry: entry[0]):
            _, ring, step, arrived = entry
            if step <= ring.steps():
                came = ring.recv(step)
                ring.send(step + 1)
                arrived(step, came)
                entry[2] += 1

    def second_z(step, came):
        if step == az.steps():
            sibling.hand(functools.partial(item_piece, 0, whole, whole, None))

    def second_y(zz, is_last):
        def arrived(step, came):
            for n, h in came if is_last else []:
                sibling.hand(functools.partial(item_piece, 1, n, whole, h))

        start(2, Ring(net, ny, y, along_y, lambda n, h: item_piece(1, n, zz, h)), arrived)

    def first_y(step, came):
        if step == ay.steps():
            start(1, az, second_z)

    def first_z(step, came):
        for n, chunk in enumerate(came):
            second_y(chunk, step == bz.steps() and n == len(came) - 1)
        if step == bz.steps():
            sibling.hand(functools.partial(item_piece, 1, y, whole, None))

    def couple(chunk, begin):
        @pl.loop(0, row_tiles)
        def _(r):
            pair = jnp.concatenate([users[0, chunk, r], users[1, chunk, r]], axis=1)
            product = jnp.dot(pair, ig[chunk], preferred_element_type=jnp.float32)
            coupled[r] = product if begin else coupled[r] + product

    ay = Direct(net, ny, y, along_y, lambda n, h: item_piece(0, n, z, h))
    bz = Direct(net, nz, z, along_z, lambda n, h: item_piece(1, y, n, h))
    az = Ring(net, nz, z, along_z, lambda n, h: item_piece(0, whole, n, h))
    start(0, ay, first_y)
    start(0, bz, first_z)
    second_y(z, bz.steps() == 0)
    if ay.steps() == 0:
        start(1, az, second_z)
    waves = max(ay.steps() + az.steps(), bz.steps() + ny // 2)
    user_hands = []
    met = xu_step = 0
    for number in range(1, waves + 1):
        wave()
        if number == 1:
            sibling.wait(own_users)
            couple(x, True)
        if number in (2, 4) and xu_step < xu.steps():
            xu_step += 1
            came = xu.recv(xu_step)
            xu.send(xu_step + 1)
            user_hands.append((came, pass_on(xu, came)))
        if number == 3 and user_hands and 2 < nx:
            came, hands = user_hands[0]
            for (chunk, _), hand in zip(came, hands):
                sibling.wait(hand)
                couple(chunk, False)
            met = 1
    while xu_step < xu.steps():
        xu_step += 1
        came = xu.recv(xu_step)
        xu.send(xu_step + 1)
        user_hands.append((came, pass_on(xu, came)))
    for step, (came, hands) in enumerate(user_hands):
        if step >= met:
            for hand in hands:
                sibling.wait(hand)
            for chunk in [came[0][0]] if step == xu.steps() - 1 else [n for n, _ in came]:
                couple(chunk, False)
    sibling.collect()
    own[2].wait()

    def whole_rank(table, row):
        return jnp.concatenate([table[kk, xx, row] for xx in range(nx) for kk in range(2)], axis=1)

    def panel_block(kk, xx, py, pz):
        return items[kk, xx, py, pl.ds(pz, 2)].reshape(tile, width)

    def error_tile(table, i):
        row, py, pz = meta[1, i], meta[2, i], meta[3, i]
        panel = jnp.concatenate([panel_block(kk, xx, py, pz) for xx in range(nx) for kk in range(2)], axis=1)
        prediction = lax.dot_general(
            whole_rank(table, row), panel, (((1,), (1,)), ((), ())), preferred_element_type=jnp.float32
        )
        live = meta[4, i].astype(jnp.float32)
        return (live * (ratings[meta[0, i]].astype(jnp.float32) - prediction)).astype(jnp.bfloat16)

    @pl.loop(0, slots, unroll=UNROLL)
    def _(i):
        errors[i] = error_tile(users, i)

    running[...] = jnp.zeros_like(running)

    @pl.loop(0, slots, unroll=UNROLL)
    def _(i):
        block = panel_block(k, x, meta[2, i], meta[3, i])
        added = jnp.dot(errors[i], block, preferred_element_type=jnp.float32)
        total = running[...] * meta[5, i].astype(jnp.float32) + added
        running[...] = total
        sums[i] = total

    def newton(factors, gradient, inverse):
        update = jnp.dot(gradient, inverse, precision=HIGHEST, preferred_element_type=jnp.float32)
        return (factors + update).astype(jnp.bfloat16)

    per = row_tiles // PARTS
    rings = []
    out_copies = []
    for part in range(PARTS):

        @pl.loop(part * per, (part + 1) * per)
        def _(r):
            observed = sums[meta[9, r]] * meta[10, r].astype(jnp.float32)
            factors = users[k, x, r].astype(jnp.float32)
            gradient = observed - UNOBSERVED * coupled[r] - REGULAR * factors
            news[k, x, r] = newton(factors, gradient, ui[...])

        def piece(chunk, half, kk=None, part=part):
            kk = k if kk is None else kk
            if half is None:
                return news.at[kk, chunk, pl.ds(part * per, per)]
            return news.at[kk, chunk, pl.ds(part * per, per), pl.ds(half * (tile // 2), tile // 2)]

        ring = Ring(net, nx, x, along_x, piece)
        ring.send(1)
        sibling.hand(functools.partial(piece, x, None))
        rings.append(ring)
        copy = pltpu.make_async_copy(
            news.at[k, x, pl.ds(part * per, per)], unew_out.at[pl.ds(part * per, per)], local_sem.at[3 + part]
        )
        copy.start()
        out_copies.append(copy)
    mine = jnp.concatenate([items[kk, xx, y, z] for xx in range(nx) for kk in range(2)], axis=1)
    icoupled[...] = jnp.dot(mine, ug[...], preferred_element_type=jnp.float32)

    for step in range(1, nx // 2 + 1):
        for ring in rings:
            came = ring.recv(step)
            ring.send(step + 1)
            pass_on(ring, came)
    sibling.collect()

    @pl.loop(0, slots, unroll=UNROLL)
    def _(i):
        errors[i] = error_tile(news, i)

    running[...] = jnp.zeros_like(running)

    @pl.loop(0, slots, unroll=UNROLL)
    def _(i):
        added = lax.dot_general(
            errors[meta[6, i]],
            news[k, x, meta[7, i]],
            (((0,), (0,)), ((), ())),
            preferred_element_type=jnp.float32,
        )
        total = running[...] * meta[8, i].astype(jnp.float32) + added
        running[...] = total
        sums[i] = total

    @pl.loop(0, panels)
    def _(p):
        panel = sums[meta[11, p]] * meta[12, p].astype(jnp.float32)
        pair = panel.astype(jnp.bfloat16).reshape(2, owner_rows, width)
        qs[lax.div(p, nz // 2), pl.ds(2 * lax.rem(p, nz // 2), 2)] = pair

    na = ra.shape[2]
    a_rows, b_rows = pl.ds(0, na), pl.ds(na, owner_rows - na)
    b_slots = [net.slot() for _ in range(1, ny)]
    a_slots = [net.slot() for _ in range(1, nz)]
    for step in range(1, ny):
        to = lax.rem(y + step, ny)
        net.push(b_slots[step - 1], qs.at[to, :, b_rows], rb.at[step - 1], along_y(step))
    for step in range(1, nz):
        to = lax.rem(z + step, nz)
        net.push(a_slots[step - 1], qs.at[:, to, a_rows], ra.at[step - 1], along_z(step))
    for step in range(1, nz):
        net.land(a_slots[step - 1], ra.at[step - 1], along_z(step))
    total = qs[:, z, a_rows].astype(jnp.float32)
    for step in range(1, nz):
        total = total + ra[step - 1].astype(jnp.float32)
    sa[...] = total.astype(jnp.bfloat16)
    c_slots = [net.slot() for _ in range(1, ny)]
    for step in range(1, ny):
        to = lax.rem(y + step, ny)
        net.push(c_slots[step - 1], sa.at[to], ta.at[step - 1], along_y(step))
    for step in range(1, ny):
        net.land(b_slots[step - 1], rb.at[step - 1], along_y(step))
    total = qs[y, :, b_rows].astype(jnp.float32)
    for step in range(1, ny):
        total = total + rb[step - 1].astype(jnp.float32)
    sb[...] = total.astype(jnp.bfloat16)
    d_slots = [net.slot() for _ in range(1, nz)]
    for step in range(1, nz):
        to = lax.rem(z + step, nz)
        net.push(d_slots[step - 1], sb.at[to], tb.at[step - 1], along_z(step))
    for step in range(1, ny):
        net.land(c_slots[step - 1], ta.at[step - 1], along_y(step))
    total_a = sa[y].astype(jnp.float32)
    for step in range(1, ny):
        total_a = total_a + ta[step - 1].astype(jnp.float32)
    for step in range(1, nz):
        net.land(d_slots[step - 1], tb.at[step - 1], along_z(step))
    total_b = sb[z].astype(jnp.float32)
    for step in range(1, nz):
        total_b = total_b + tb[step - 1].astype(jnp.float32)
    observed = jnp.concatenate([total_a, total_b], axis=0)
    factors = items[k, x, y, z].astype(jnp.float32)
    gradient = observed - UNOBSERVED * icoupled[...] - REGULAR * factors
    inew_out[...] = newton(factors, gradient, ii[...])
    for copy in out_copies:
        copy.wait()
    net.drain()


def lookup(tile_coords, tile_count, row_tiles, panel_count, nz):
    count = tile_coords.shape[0]
    row, panel = tile_coords[:, 0], tile_coords[:, 1]
    slot = lax.iota(jnp.int32, count)
    live = (slot < tile_count[0]).astype(jnp.int32)

    def rank_of(value):
        key = value * count + slot
        return jnp.sum((key[None, :] < key[:, None]).astype(jnp.int32), axis=1)

    def sort_by(rank, value):
        return jnp.sum(jnp.where(rank[None, :] == slot[:, None], value[None, :], 0), axis=1)

    def same(value):
        return jnp.concatenate([jnp.zeros((1,), jnp.int32), (value[1:] == value[:-1]).astype(jnp.int32)])

    def last(value, size):
        ids = lax.iota(jnp.int32, size)[:, None]
        upto = jnp.sum((value[None, :] <= ids).astype(jnp.int32), axis=1)
        has = jnp.any(value[None, :] == ids, axis=1).astype(jnp.int32)
        return jnp.maximum(upto - 1, 0), has

    by_row, by_panel = rank_of(row), rank_of(panel)
    sorted_row, sorted_panel = sort_by(by_row, row), sort_by(by_row, panel)
    last_row, has_row = last(row, row_tiles)
    last_panel, has_panel = last(panel, panel_count)
    lines = [
        sort_by(by_row, slot),
        sorted_row,
        sorted_panel // (nz // 2),
        2 * (sorted_panel % (nz // 2)),
        sort_by(by_row, live),
        same(sorted_row),
        sort_by(by_panel, by_row),
        sort_by(by_panel, row),
        same(sort_by(by_panel, panel)),
        last_row,
        has_row,
        last_panel,
        has_panel,
    ]
    wide = max(count, row_tiles, panel_count)
    return jnp.stack([jnp.pad(line, (0, wide - line.shape[0])) for line in lines])


def local(nx, nz, user_factors, item_factors, ratings, tile_coords, tile_count, item_gram, user_gram, user_inverse, item_inverse):
    user_rows, width = user_factors.shape
    owner_rows = item_factors.shape[0]
    slots, tile, _ = ratings.shape
    row_tiles = user_rows // tile
    panel_count = NY * nz * owner_rows // tile
    meta = lookup(tile_coords, tile_count, row_tiles, panel_count, nz)
    na = owner_rows * 3 // 8 // 16 * 16
    nb = owner_rows - na
    bf16, f32 = jnp.bfloat16, jnp.float32
    vmem = pl.BlockSpec(memory_space=pltpu.VMEM)
    hbm = pl.BlockSpec(memory_space=pl.ANY)
    user_new, item_new = pl.pallas_call(
        functools.partial(kernel, nx, nz),
        out_shape=(
            jax.ShapeDtypeStruct((row_tiles, tile, width), bf16),
            jax.ShapeDtypeStruct((owner_rows, width), bf16),
        ),
        in_specs=[pl.BlockSpec(memory_space=pltpu.SMEM), hbm, hbm, hbm, vmem, vmem, vmem, vmem],
        out_specs=(hbm, vmem),
        scratch_shapes=[
            pltpu.VMEM((2, nx, row_tiles, tile, width), bf16),
            pltpu.VMEM((2, nx, NY, nz, owner_rows, width), bf16),
            pltpu.VMEM((2, nx, row_tiles, tile, width), bf16),
            pltpu.VMEM((slots, tile, tile), bf16),
            pltpu.VMEM((slots, tile, tile), bf16),
            pltpu.VMEM((slots, tile, width), f32),
            pltpu.VMEM((tile, width), f32),
            pltpu.VMEM((row_tiles, tile, width), f32),
            pltpu.VMEM((owner_rows, width), f32),
            pltpu.VMEM((NY, nz, owner_rows, width), bf16),
            pltpu.VMEM((nz - 1, NY, na, width), bf16),
            pltpu.VMEM((NY, na, width), bf16),
            pltpu.VMEM((max(NY - 1, 1), na, width), bf16),
            pltpu.VMEM((max(NY - 1, 1), nz, nb, width), bf16),
            pltpu.VMEM((nz, nb, width), bf16),
            pltpu.VMEM((nz - 1, nb, width), bf16),
            pltpu.SemaphoreType.DMA((SEMS,)),
            pltpu.SemaphoreType.DMA((SEMS,)),
            pltpu.SemaphoreType.DMA((3 + PARTS,)),
        ],
        compiler_params=pltpu.CompilerParams(
            collective_id=0, has_side_effects=True, vmem_limit_bytes=56 * 1024 * 1024
        ),
    )(
        meta,
        user_factors.reshape(row_tiles, tile, width),
        item_factors,
        ratings,
        item_gram.reshape(nx, 2 * width, width),
        user_gram,
        user_inverse,
        item_inverse,
    )
    return user_new.reshape(user_rows, width), item_new


def solution(mesh):
    placed = (
        P("users", "dims"),
        P("users", "dims"),
        P("users", None, None),
        P("users", None),
        P("users"),
        P(None, "dims"),
        P(None, "dims"),
        P("dims", None),
        P("dims", None),
    )
    return jax.shard_map(
        functools.partial(local, mesh.shape["dims"] // 2, mesh.shape["users"] // NY),
        mesh=mesh,
        in_specs=placed,
        out_specs=(P("users", "dims"), P("users", "dims")),
        check_vma=False,
    )
```

```python
import functools

import jax
import jax.numpy as jnp
from jax import lax
from jax.experimental import pallas as pl
from jax.experimental.pallas import tpu as pltpu
from jax.sharding import PartitionSpec as P

UNOBSERVED = 256.0
REGULAR = 2.0
HIGHEST = lax.Precision.HIGHEST
MESH = pl.DeviceIdType.MESH
NY = 4
PARTS = 4
SEMS = 240
UNROLL = 5


class Net:
    def __init__(self, send_sem, recv_sem):
        self.send_sem = send_sem
        self.recv_sem = recv_sem
        self.used = 0
        self.started = []

    def slot(self):
        self.used += 1
        return self.used - 1

    def push(self, index, source, target, device):
        copy = pltpu.make_async_remote_copy(
            src_ref=source,
            dst_ref=target,
            send_sem=self.send_sem.at[index],
            recv_sem=self.recv_sem.at[index],
            device_id=device,
            device_id_type=MESH,
        )
        copy.start()
        self.started.append(copy)

    def land(self, index, target, device):
        pltpu.make_async_remote_copy(
            src_ref=target,
            dst_ref=target,
            send_sem=self.send_sem.at[index],
            recv_sem=self.recv_sem.at[index],
            device_id=device,
            device_id_type=MESH,
        ).wait_recv()

    def drain(self):
        for copy in self.started:
            copy.wait_send()
        self.started = []


class Ring:
    def __init__(self, net, size, place, to, piece):
        self.net, self.size, self.place, self.to, self.piece = net, size, place, to, piece
        self.slots = {}
        for distance in range(1, size // 2 + 1):
            self.slots[distance] = (net.slot(), net.slot())

    def steps(self):
        return self.size // 2

    def halves(self, distance):
        return (0, 1) if 2 * distance == self.size else (None, None)

    def send(self, distance):
        if distance > self.steps():
            return
        for index, step, half in zip(self.slots[distance], (1, -1), self.halves(distance)):
            chunk = lax.rem(self.place - step * (distance - 1) + self.size, self.size)
            view = self.piece(chunk, half)
            self.net.push(index, view, view, self.to(step))

    def recv(self, distance):
        if distance > self.steps():
            return []
        came = []
        for index, step, half in zip(self.slots[distance], (1, -1), self.halves(distance)):
            chunk = lax.rem(self.place - step * distance + self.size, self.size)
            self.net.land(index, self.piece(chunk, half), self.to(step))
            came.append((chunk, half))
        return came


class Shift(Ring):
    def send(self, distance):
        if distance > self.steps():
            return
        for index, step, half in zip(self.slots[distance], (1, -1), self.halves(distance)):
            here, there = -step * (distance - 1) % self.size, -step * distance % self.size
            self.net.push(index, self.piece(here, half), self.piece(there, half), self.to(step))

    def recv(self, distance):
        came = []
        for index, step, half in zip(self.slots[distance], (1, -1), self.halves(distance)):
            back = -step * distance % self.size
            self.net.land(index, self.piece(back, half), self.to(step))
            came.append((back, half))
        return came


class Direct:
    def __init__(self, net, size, place, to, piece):
        self.net, self.size, self.place, self.to, self.piece = net, size, place, to, piece
        near = [step for step in (1, -1, 2, -2) if abs(step) < size]
        near = [step for n, step in enumerate(near) if step % size not in [e % size for e in near[:n]]]
        self.plan = [[(net.slot(), 0, step, None) for step in near]] if near else []
        if size == 8:
            self.plan.append([(net.slot(), 2, 1, None), (net.slot(), -2, -1, None), (net.slot(), 2, 2, 0), (net.slot(), -2, -2, 1)])

    def steps(self):
        return len(self.plan)

    def chunk(self, back):
        return lax.rem(self.place - back + self.size, self.size)

    def send(self, step):
        if step > self.steps():
            return
        for index, back, jump, half in self.plan[step - 1]:
            view = self.piece(self.chunk(back), half)
            self.net.push(index, view, view, self.to(jump))

    def recv(self, step):
        came = []
        for index, back, jump, half in self.plan[step - 1]:
            chunk = self.chunk(back + jump)
            self.net.land(index, self.piece(chunk, half), self.to(jump))
            if half != 0:
                came.append(chunk)
        return came


class Sibling:
    def __init__(self, net, core, device):
        self.net, self.core, self.device = net, core, device
        self.due = {}

    def hand(self, piece):
        index = self.net.slot()
        view = piece(self.core)
        self.net.push(index, view, view, self.device)
        self.due[index] = piece
        return index

    def wait(self, index):
        self.net.land(index, self.due.pop(index)(1 - self.core), self.device)

    def collect(self):
        for index in list(self.due):
            self.wait(index)


def lookup(coords, count, lines):
    slots = coords.shape[1]
    low = lax.broadcasted_iota(jnp.int32, (slots, slots), 0)
    high = lax.broadcasted_iota(jnp.int32, (slots, slots), 1)

    def down(flat):
        return jnp.sum(jnp.where(low == high, flat, 0), axis=1, keepdims=True)

    def pick(rank, value):
        return jnp.sum(jnp.where(rank == high, value, 0), axis=0, keepdims=True)

    row, panel = coords[0:1, :], coords[1:2, :]
    row_down, panel_down = down(row), down(panel)
    live = (low < count).astype(jnp.int32)

    def rank_of(flat, tall):
        return jnp.sum((flat * slots + high < tall * slots + low).astype(jnp.int32), axis=1, keepdims=True)

    by_row, by_panel = rank_of(row, row_down), rank_of(panel, panel_down)

    def same(rank, value):
        first = lax.broadcasted_iota(jnp.int32, (1, slots), 1) > 0
        return ((pick(rank, value) == pick(rank + 1, value)) & first).astype(jnp.int32)

    def last(value):
        upto = jnp.sum((value <= high).astype(jnp.int32), axis=0, keepdims=True)
        has = jnp.sum((value == high).astype(jnp.int32), axis=0, keepdims=True)
        return jnp.maximum(upto - 1, 0), jnp.minimum(has, 1)

    found = [
        pick(by_row, low),
        pick(by_row, row_down),
        pick(by_row, panel_down),
        pick(by_row, live),
        same(by_row, row_down),
        pick(by_panel, by_row),
        pick(by_panel, row_down),
        same(by_panel, panel_down),
        *last(row_down),
        *last(panel_down),
    ]
    for n, line in enumerate(found):
        lines[n : n + 1, 0:slots] = line


def kernel(
    nx, nz, coords, count, u_hbm, i_hbm, r_hbm, ig, ug, ui, ii, unew_out, inew_out,
    lines, meta, users, items, news_0, news_1, news_2, news_3, ratings, predicted, errors, sums, running, coupled, icoupled,
    qs, ra, sa, ta, rb, sb, tb, send_sem, recv_sem, local_sem,
):
    ny = NY
    u = lax.axis_index("users")
    c = lax.axis_index("dims")
    y, z = lax.div(u, nz), lax.rem(u, nz)
    x, k = lax.div(c, 2), lax.rem(c, 2)

    def device(xx, kk, yy, zz):
        return (yy * nz + zz, xx * 2 + kk)

    def along_x(step):
        return device(lax.rem(x + step + nx, nx), k, y, z)

    def along_y(step):
        return device(x, k, lax.rem(y + step + ny, ny), z)

    def along_z(step):
        return device(x, k, y, lax.rem(z + step + nz, nz))

    other_core = device(x, 1 - k, y, z)
    row_tiles, tile, width = users.shape[2:]
    slots = ratings.shape[0]
    panels = ny * nz // 2

    own = [
        pltpu.make_async_copy(i_hbm, items.at[k, x, y, z], local_sem.at[0]),
        pltpu.make_async_copy(u_hbm, users.at[k, x], local_sem.at[1]),
        pltpu.make_async_copy(r_hbm, ratings, local_sem.at[2]),
    ]
    for copy in own:
        copy.start()

    barrier = pltpu.get_barrier_semaphore()
    peers = [along_x(s) for s in range(1, nx)]
    peers += [along_y(s) for s in range(1, ny)]
    peers += [along_z(s) for s in range(1, nz)]
    peers += [other_core]
    for peer in peers:
        pl.semaphore_signal(barrier, inc=1, device_id=peer, device_id_type=MESH)
    lookup(coords, count[0], lines)
    to_scalars = pltpu.make_async_copy(lines, meta, local_sem.at[3 + PARTS])
    to_scalars.start()
    pl.semaphore_wait(barrier, len(peers))

    net = Net(send_sem, recv_sem)
    sibling = Sibling(net, k, other_core)
    own[0].wait()
    own[1].wait()

    first = [net.slot() for _ in range(1, nx)]
    for index, step in zip(first, range(1, nx)):
        view = items.at[k, x, y, z]
        net.push(index, view, view, along_x(step))

    half_rows = row_tiles // 2

    def user_piece(table):
        def piece(chunk, half, kk=None):
            kk = k if kk is None else kk
            if half is None:
                return table.at[kk, chunk]
            return table.at[kk, chunk, pl.ds(half * half_rows, half_rows)]

        return piece

    xu = Ring(net, nx, x, along_x, user_piece(users))
    xu.send(1)
    own_users = sibling.hand(lambda kk: users.at[kk, x])
    for index, step in zip(first, range(1, nx)):
        source = lax.rem(x - step + nx, nx)
        net.land(index, items.at[k, source, y, z], along_x(step))

    owner_rows = items.shape[4]
    split = owner_rows * 3 // 8 // 16 * 16

    def blocks(half):
        if half is None or nx < 2:
            return pl.ds(0, nx)
        return pl.ds(half * (nx // 2), nx // 2)

    def rows_of(part, half):
        low, size = (split, owner_rows - split) if part else (0, split)
        if half is None or nx >= 2:
            return pl.ds(low, size)
        return pl.ds(low + half * (size // 2), size // 2)

    def item_piece(part, yy, zz, half, kk=None):
        return items.at[k if kk is None else kk, blocks(half), yy, zz, rows_of(part, half)]

    def pass_on(ring, came):
        return [sibling.hand(functools.partial(ring.piece, chunk, half)) for chunk, half in came]

    active = []
    whole = slice(None)

    def start(order, ring, arrived):
        ring.send(1)
        active.append([order, ring, 1, arrived])

    def wave():
        for entry in sorted(active, key=lambda entry: entry[0]):
            _, ring, step, arrived = entry
            if step <= ring.steps():
                came = ring.recv(step)
                ring.send(step + 1)
                arrived(step, came)
                entry[2] += 1

    def second_z(step, came):
        if step == az.steps():
            sibling.hand(functools.partial(item_piece, 0, whole, whole, None))

    def second_y(zz, is_last):
        def arrived(step, came):
            for n, h in came if is_last else []:
                sibling.hand(functools.partial(item_piece, 1, n, whole, h))

        start(2, Ring(net, ny, y, along_y, lambda n, h: item_piece(1, n, zz, h)), arrived)

    def first_y(step, came):
        if step == ay.steps():
            start(1, az, second_z)

    def first_z(step, came):
        for n, chunk in enumerate(came):
            second_y(chunk, step == bz.steps() and n == len(came) - 1)
        if step == bz.steps():
            sibling.hand(functools.partial(item_piece, 1, y, whole, None))

    def couple(chunk, begin):
        @pl.loop(0, row_tiles)
        def _(r):
            pair = jnp.concatenate([users[0, chunk, r], users[1, chunk, r]], axis=1)
            product = jnp.dot(pair, ig[chunk], preferred_element_type=jnp.float32)
            coupled[r] = product if begin else coupled[r] + product

    ay = Direct(net, ny, y, along_y, lambda n, h: item_piece(0, n, z, h))
    bz = Direct(net, nz, z, along_z, lambda n, h: item_piece(1, y, n, h))
    az = Ring(net, nz, z, along_z, lambda n, h: item_piece(0, whole, n, h))
    start(0, ay, first_y)
    start(0, bz, first_z)
    second_y(z, bz.steps() == 0)
    if ay.steps() == 0:
        start(1, az, second_z)
    waves = max(ay.steps() + az.steps(), bz.steps() + ny // 2)
    user_hands = []
    met = xu_step = 0
    for number in range(1, waves + 1):
        wave()
        if number == 1:
            sibling.wait(own_users)
            couple(x, True)
        if number in (2, 4) and xu_step < xu.steps():
            xu_step += 1
            came = xu.recv(xu_step)
            xu.send(xu_step + 1)
            user_hands.append((came, pass_on(xu, came)))
        if number == 3 and user_hands and 2 < nx:
            came, hands = user_hands[0]
            for (chunk, _), hand in zip(came, hands):
                sibling.wait(hand)
                couple(chunk, False)
            met = 1
    while xu_step < xu.steps():
        xu_step += 1
        came = xu.recv(xu_step)
        xu.send(xu_step + 1)
        user_hands.append((came, pass_on(xu, came)))
    for step, (came, hands) in enumerate(user_hands):
        if step >= met:
            for hand in hands:
                sibling.wait(hand)
            for chunk in [came[0][0]] if step == xu.steps() - 1 else [n for n, _ in came]:
                couple(chunk, False)
    sibling.collect()
    own[2].wait()
    to_scalars.wait()

    def panel_block(kk, xx, i):
        panel = meta[2, i]
        return items[kk, xx, lax.div(panel, nz // 2), pl.ds(2 * lax.rem(panel, nz // 2), 2)].reshape(tile, width)

    def product(user_blocks, chunks, i):
        panel = jnp.concatenate([panel_block(kk, xx, i) for xx in chunks for kk in range(2)], axis=1)
        return lax.dot_general(
            jnp.concatenate(user_blocks, axis=1), panel, (((1,), (1,)), ((), ())), preferred_element_type=jnp.float32
        )

    def error_of(prediction, i):
        live = meta[3, i].astype(jnp.float32)
        return (live * (ratings[meta[0, i]].astype(jnp.float32) - prediction)).astype(jnp.bfloat16)

    @pl.loop(0, slots, unroll=UNROLL)
    def _(i):
        row = meta[1, i]
        blocks_of_users = [users[kk, xx, row] for xx in range(nx) for kk in range(2)]
        errors[i] = error_of(product(blocks_of_users, range(nx), i), i)

    running[...] = jnp.zeros_like(running)

    @pl.loop(0, slots, unroll=UNROLL)
    def _(i):
        added = jnp.dot(errors[i], panel_block(k, x, i), preferred_element_type=jnp.float32)
        total = running[...] * meta[4, i].astype(jnp.float32) + added
        running[...] = total
        sums[i] = total

    def newton(factors, gradient, inverse):
        update = jnp.dot(gradient, inverse, precision=HIGHEST, preferred_element_type=jnp.float32)
        return (factors + update).astype(jnp.bfloat16)

    per = row_tiles // PARTS
    rings = []
    own_news = []
    news = [news_0, news_1, news_2, news_3]
    out_copies = []
    for part in range(PARTS):

        @pl.loop(part * per, (part + 1) * per)
        def _(r):
            observed = sums[meta[8, r]] * meta[9, r].astype(jnp.float32)
            factors = users[k, x, r].astype(jnp.float32)
            gradient = observed - UNOBSERVED * coupled[r] - REGULAR * factors
            news[0][k, r] = newton(factors, gradient, ui[...])

        def piece(back, half, kk=None, part=part):
            kk = k if kk is None else kk
            if half is None:
                return news[back].at[kk, pl.ds(part * per, per)]
            return news[back].at[kk, pl.ds(part * per, per), pl.ds(half * (tile // 2), tile // 2)]

        ring = Shift(net, nx, x, along_x, piece)
        ring.send(1)
        own_news.append(sibling.hand(functools.partial(piece, 0, None)))
        rings.append(ring)
        copy = pltpu.make_async_copy(
            news[0].at[k, pl.ds(part * per, per)], unew_out.at[pl.ds(part * per, per)], local_sem.at[3 + part]
        )
        copy.start()
        out_copies.append(copy)
    mine = jnp.concatenate([items[kk, xx, y, z] for xx in range(nx) for kk in range(2)], axis=1)
    icoupled[...] = jnp.dot(mine, ug[...], preferred_element_type=jnp.float32)

    def predict_from(backs, begin, end):
        @pl.loop(0, slots, unroll=UNROLL)
        def _(i):
            row = meta[1, i]
            blocks_of_users = [news[back][kk, row] for back in backs for kk in range(2)]
            value = product(blocks_of_users, [lax.rem(x + back, nx) for back in backs], i)
            value = value if begin else predicted[i] + value
            if end:
                errors[i] = error_of(value, i)
            else:
                predicted[i] = value

    hands = own_news
    for step in range(nx // 2 + 1):
        if step > 0:
            hands = []
            for ring in rings:
                came = ring.recv(step)
                ring.send(step + 1)
                hands += pass_on(ring, came)
        for hand in hands:
            sibling.wait(hand)
        predict_from(sorted({step, (nx - step) % nx}), step == 0, step == nx // 2)

    running[...] = jnp.zeros_like(running)

    @pl.loop(0, slots, unroll=UNROLL)
    def _(i):
        added = lax.dot_general(
            errors[meta[5, i]],
            news[0][k, meta[6, i]],
            (((0,), (0,)), ((), ())),
            preferred_element_type=jnp.float32,
        )
        total = running[...] * meta[7, i].astype(jnp.float32) + added
        running[...] = total
        sums[i] = total

    @pl.loop(0, panels)
    def _(p):
        panel = sums[meta[10, p]] * meta[11, p].astype(jnp.float32)
        pair = panel.astype(jnp.bfloat16).reshape(2, owner_rows, width)
        qs[lax.div(p, nz // 2), pl.ds(2 * lax.rem(p, nz // 2), 2)] = pair

    na = ra.shape[2]
    a_rows, b_rows = pl.ds(0, na), pl.ds(na, owner_rows - na)
    b_slots = [net.slot() for _ in range(1, ny)]
    a_slots = [net.slot() for _ in range(1, nz)]
    for step in range(1, ny):
        to = lax.rem(y + step, ny)
        net.push(b_slots[step - 1], qs.at[to, :, b_rows], rb.at[step - 1], along_y(step))
    for step in range(1, nz):
        to = lax.rem(z + step, nz)
        net.push(a_slots[step - 1], qs.at[:, to, a_rows], ra.at[step - 1], along_z(step))
    for step in range(1, nz):
        net.land(a_slots[step - 1], ra.at[step - 1], along_z(step))
    total = qs[:, z, a_rows].astype(jnp.float32)
    for step in range(1, nz):
        total = total + ra[step - 1].astype(jnp.float32)
    sa[...] = total.astype(jnp.bfloat16)
    c_slots = [net.slot() for _ in range(1, ny)]
    for step in range(1, ny):
        to = lax.rem(y + step, ny)
        net.push(c_slots[step - 1], sa.at[to], ta.at[step - 1], along_y(step))
    for step in range(1, ny):
        net.land(b_slots[step - 1], rb.at[step - 1], along_y(step))
    total = qs[y, :, b_rows].astype(jnp.float32)
    for step in range(1, ny):
        total = total + rb[step - 1].astype(jnp.float32)
    sb[...] = total.astype(jnp.bfloat16)
    d_slots = [net.slot() for _ in range(1, nz)]
    for step in range(1, nz):
        to = lax.rem(z + step, nz)
        net.push(d_slots[step - 1], sb.at[to], tb.at[step - 1], along_z(step))
    for step in range(1, ny):
        net.land(c_slots[step - 1], ta.at[step - 1], along_y(step))
    total_a = sa[y].astype(jnp.float32)
    for step in range(1, ny):
        total_a = total_a + ta[step - 1].astype(jnp.float32)
    for step in range(1, nz):
        net.land(d_slots[step - 1], tb.at[step - 1], along_z(step))
    total_b = sb[z].astype(jnp.float32)
    for step in range(1, nz):
        total_b = total_b + tb[step - 1].astype(jnp.float32)
    observed = jnp.concatenate([total_a, total_b], axis=0)
    factors = items[k, x, y, z].astype(jnp.float32)
    gradient = observed - UNOBSERVED * icoupled[...] - REGULAR * factors
    inew_out[...] = newton(factors, gradient, ii[...])
    for copy in out_copies:
        copy.wait()
    net.drain()


def local(nx, nz, user_factors, item_factors, ratings, tile_coords, tile_count, item_gram, user_gram, user_inverse, item_inverse):
    user_rows, width = user_factors.shape
    owner_rows = item_factors.shape[0]
    slots, tile, _ = ratings.shape
    row_tiles = user_rows // tile
    na = owner_rows * 3 // 8 // 16 * 16
    nb = owner_rows - na
    bf16, f32 = jnp.bfloat16, jnp.float32
    vmem = pl.BlockSpec(memory_space=pltpu.VMEM)
    hbm = pl.BlockSpec(memory_space=pl.ANY)
    user_new, item_new = pl.pallas_call(
        functools.partial(kernel, nx, nz),
        out_shape=(
            jax.ShapeDtypeStruct((row_tiles, tile, width), bf16),
            jax.ShapeDtypeStruct((owner_rows, width), bf16),
        ),
        in_specs=[vmem, pl.BlockSpec(memory_space=pltpu.SMEM), hbm, hbm, hbm, vmem, vmem, vmem, vmem],
        out_specs=(hbm, vmem),
        scratch_shapes=[
            pltpu.VMEM((16, 128), jnp.int32),
            pltpu.SMEM((16, 128), jnp.int32),
            pltpu.VMEM((2, nx, row_tiles, tile, width), bf16),
            pltpu.VMEM((2, nx, NY, nz, owner_rows, width), bf16),
            *[pltpu.VMEM((2, row_tiles, tile, width), bf16)] * 4,
            pltpu.VMEM((slots, tile, tile), bf16),
            pltpu.VMEM((slots, tile, tile), f32),
            pltpu.VMEM((slots, tile, tile), bf16),
            pltpu.VMEM((slots, tile, width), f32),
            pltpu.VMEM((tile, width), f32),
            pltpu.VMEM((row_tiles, tile, width), f32),
            pltpu.VMEM((owner_rows, width), f32),
            pltpu.VMEM((NY, nz, owner_rows, width), bf16),
            pltpu.VMEM((nz - 1, NY, na, width), bf16),
            pltpu.VMEM((NY, na, width), bf16),
            pltpu.VMEM((max(NY - 1, 1), na, width), bf16),
            pltpu.VMEM((max(NY - 1, 1), nz, nb, width), bf16),
            pltpu.VMEM((nz, nb, width), bf16),
            pltpu.VMEM((nz - 1, nb, width), bf16),
            pltpu.SemaphoreType.DMA((SEMS,)),
            pltpu.SemaphoreType.DMA((SEMS,)),
            pltpu.SemaphoreType.DMA((4 + PARTS,)),
        ],
        compiler_params=pltpu.CompilerParams(
            collective_id=0, has_side_effects=True, vmem_limit_bytes=56 * 1024 * 1024
        ),
    )(
        tile_coords.T,
        tile_count,
        user_factors.reshape(row_tiles, tile, width),
        item_factors,
        ratings,
        item_gram.reshape(nx, 2 * width, width),
        user_gram,
        user_inverse,
        item_inverse,
    )
    return user_new.reshape(user_rows, width), item_new


def solution(mesh):
    placed = (
        P("users", "dims"),
        P("users", "dims"),
        P("users", None, None),
        P("users", None),
        P("users"),
        P(None, "dims"),
        P(None, "dims"),
        P("dims", None),
        P("dims", None),
    )
    return jax.shard_map(
        functools.partial(local, mesh.shape["dims"] // 2, mesh.shape["users"] // NY),
        mesh=mesh,
        in_specs=placed,
        out_specs=(P("users", "dims"), P("users", "dims")),
        check_vma=False,
    )
```

```python
import functools

import jax
import jax.numpy as jnp
from jax import lax
from jax.experimental import pallas as pl
from jax.experimental.pallas import tpu as pltpu
from jax.sharding import PartitionSpec as P

UNOBSERVED = 256.0
REGULAR = 2.0
HIGHEST = lax.Precision.HIGHEST
MESH = pl.DeviceIdType.MESH
NY = 4
PARTS = 4
SEMS = 240
UNROLL = 5
LANES = 2


class Net:
    def __init__(self, send_sem, recv_sem):
        self.send_sem = send_sem
        self.recv_sem = recv_sem
        self.used = 0
        self.started = []

    def slot(self):
        self.used += 1
        return self.used - 1

    def push(self, index, source, target, device):
        copy = pltpu.make_async_remote_copy(
            src_ref=source,
            dst_ref=target,
            send_sem=self.send_sem.at[index],
            recv_sem=self.recv_sem.at[index],
            device_id=device,
            device_id_type=MESH,
        )
        copy.start()
        self.started.append(copy)

    def land(self, index, target, device):
        pltpu.make_async_remote_copy(
            src_ref=target,
            dst_ref=target,
            send_sem=self.send_sem.at[index],
            recv_sem=self.recv_sem.at[index],
            device_id=device,
            device_id_type=MESH,
        ).wait_recv()

    def drain(self):
        for copy in self.started:
            copy.wait_send()
        self.started = []


class Ring:
    def __init__(self, net, size, place, to, piece):
        self.net, self.size, self.place, self.to, self.piece = net, size, place, to, piece
        self.slots = {}
        for distance in range(1, size // 2 + 1):
            self.slots[distance] = (net.slot(), net.slot())

    def steps(self):
        return self.size // 2

    def halves(self, distance):
        return (0, 1) if 2 * distance == self.size else (None, None)

    def send(self, distance):
        if distance > self.steps():
            return
        for index, step, half in zip(self.slots[distance], (1, -1), self.halves(distance)):
            chunk = lax.rem(self.place - step * (distance - 1) + self.size, self.size)
            view = self.piece(chunk, half)
            self.net.push(index, view, view, self.to(step))

    def recv(self, distance):
        if distance > self.steps():
            return []
        came = []
        for index, step, half in zip(self.slots[distance], (1, -1), self.halves(distance)):
            chunk = lax.rem(self.place - step * distance + self.size, self.size)
            self.net.land(index, self.piece(chunk, half), self.to(step))
            came.append((chunk, half))
        return came


class Shift(Ring):
    def send(self, distance):
        if distance > self.steps():
            return
        for index, step, half in zip(self.slots[distance], (1, -1), self.halves(distance)):
            here, there = -step * (distance - 1) % self.size, -step * distance % self.size
            self.net.push(index, self.piece(here, half), self.piece(there, half), self.to(step))

    def recv(self, distance):
        came = []
        for index, step, half in zip(self.slots[distance], (1, -1), self.halves(distance)):
            back = -step * distance % self.size
            self.net.land(index, self.piece(back, half), self.to(step))
            came.append((back, half))
        return came


class Direct:
    def __init__(self, net, size, place, to, piece):
        self.net, self.size, self.place, self.to, self.piece = net, size, place, to, piece
        near = [step for step in (1, -1, 2, -2) if abs(step) < size]
        near = [step for n, step in enumerate(near) if step % size not in [e % size for e in near[:n]]]
        self.plan = [[(net.slot(), 0, step, None) for step in near]] if near else []
        if size == 8:
            self.plan.append([(net.slot(), 2, 1, None), (net.slot(), -2, -1, None), (net.slot(), 2, 2, 0), (net.slot(), -2, -2, 1)])

    def steps(self):
        return len(self.plan)

    def chunk(self, back):
        return lax.rem(self.place - back + self.size, self.size)

    def send(self, step):
        if step > self.steps():
            return
        for index, back, jump, half in self.plan[step - 1]:
            view = self.piece(self.chunk(back), half)
            self.net.push(index, view, view, self.to(jump))

    def recv(self, step):
        came = []
        for index, back, jump, half in self.plan[step - 1]:
            chunk = self.chunk(back + jump)
            self.net.land(index, self.piece(chunk, half), self.to(jump))
            if half != 0:
                came.append(chunk)
        return came


class Sibling:
    def __init__(self, net, core, device):
        self.net, self.core, self.device = net, core, device
        self.due = {}

    def hand(self, piece):
        index = self.net.slot()
        view = piece(self.core)
        self.net.push(index, view, view, self.device)
        self.due[index] = piece
        return index

    def wait(self, index):
        self.net.land(index, self.due.pop(index)(1 - self.core), self.device)

    def collect(self):
        for index in list(self.due):
            self.wait(index)


def lookup(coords, count, lines):
    slots = coords.shape[1]
    low = lax.broadcasted_iota(jnp.int32, (slots, slots), 0)
    high = lax.broadcasted_iota(jnp.int32, (slots, slots), 1)

    def down(flat):
        return jnp.sum(jnp.where(low == high, flat, 0), axis=1, keepdims=True)

    def pick(rank, value):
        return jnp.sum(jnp.where(rank == high, value, 0), axis=0, keepdims=True)

    row, panel = coords[0:1, :], coords[1:2, :]
    row_down, panel_down = down(row), down(panel)
    live = (low < count).astype(jnp.int32)

    def rank_of(flat, tall):
        return jnp.sum((flat * slots + high < tall * slots + low).astype(jnp.int32), axis=1, keepdims=True)

    by_row, by_panel = rank_of(row, row_down), rank_of(panel, panel_down)

    def same(rank, value):
        first = lax.broadcasted_iota(jnp.int32, (1, slots), 1) > 0
        return ((pick(rank, value) == pick(rank + 1, value)) & first).astype(jnp.int32)

    def last(value):
        upto = jnp.sum((value <= high).astype(jnp.int32), axis=0, keepdims=True)
        has = jnp.sum((value == high).astype(jnp.int32), axis=0, keepdims=True)
        return jnp.maximum(upto - 1, 0), jnp.minimum(has, 1)

    found = [
        pick(by_row, low),
        pick(by_row, row_down),
        pick(by_row, panel_down),
        pick(by_row, live),
        same(by_row, row_down),
        pick(by_panel, by_row),
        pick(by_panel, row_down),
        same(by_panel, panel_down),
        *last(row_down),
        *last(panel_down),
    ]
    for n, line in enumerate(found):
        lines[n : n + 1, 0:slots] = line


def kernel(
    nx, nz, coords, count, u_hbm, i_hbm, r_hbm, ig, ug, ui, ii, unew_out, inew_out,
    lines, meta, users, items, news_0, news_1, news_2, news_3, ratings, predicted, errors, sums, running, coupled, icoupled,
    qs, ra, sa, ta, rb, sb, tb, send_sem, recv_sem, local_sem,
):
    ny = NY
    u = lax.axis_index("users")
    c = lax.axis_index("dims")
    y, z = lax.div(u, nz), lax.rem(u, nz)
    x, k = lax.div(c, 2), lax.rem(c, 2)

    def device(xx, kk, yy, zz):
        return (yy * nz + zz, xx * 2 + kk)

    def along_x(step):
        return device(lax.rem(x + step + nx, nx), k, y, z)

    def along_y(step):
        return device(x, k, lax.rem(y + step + ny, ny), z)

    def along_z(step):
        return device(x, k, y, lax.rem(z + step + nz, nz))

    other_core = device(x, 1 - k, y, z)
    row_tiles, tile, width = users.shape[2:]
    slots = ratings.shape[0]
    panels = ny * nz // 2

    own = [
        pltpu.make_async_copy(i_hbm, items.at[k, x, y, z], local_sem.at[0]),
        pltpu.make_async_copy(u_hbm, users.at[k, x], local_sem.at[1]),
        pltpu.make_async_copy(r_hbm, ratings, local_sem.at[2]),
    ]
    for copy in own:
        copy.start()

    barrier = pltpu.get_barrier_semaphore()
    peers = [along_x(s) for s in range(1, nx)]
    peers += [along_y(s) for s in range(1, ny)]
    peers += [along_z(s) for s in range(1, nz)]
    peers += [other_core]
    for peer in peers:
        pl.semaphore_signal(barrier, inc=1, device_id=peer, device_id_type=MESH)
    lookup(coords, count[0], lines)
    to_scalars = pltpu.make_async_copy(lines, meta, local_sem.at[3 + PARTS])
    to_scalars.start()
    pl.semaphore_wait(barrier, len(peers))

    net = Net(send_sem, recv_sem)
    sibling = Sibling(net, k, other_core)
    own[0].wait()
    own[1].wait()

    first = [net.slot() for _ in range(1, nx)]
    for index, step in zip(first, range(1, nx)):
        view = items.at[k, x, y, z]
        net.push(index, view, view, along_x(step))

    half_rows = row_tiles // 2

    def user_piece(table):
        def piece(chunk, half, kk=None):
            kk = k if kk is None else kk
            if half is None:
                return table.at[kk, chunk]
            return table.at[kk, chunk, pl.ds(half * half_rows, half_rows)]

        return piece

    xu = Ring(net, nx, x, along_x, user_piece(users))
    xu.send(1)
    own_users = sibling.hand(lambda kk: users.at[kk, x])
    for index, step in zip(first, range(1, nx)):
        source = lax.rem(x - step + nx, nx)
        net.land(index, items.at[k, source, y, z], along_x(step))

    owner_rows = items.shape[4]
    split = owner_rows * 3 // 8 // 16 * 16

    def blocks(half):
        if half is None or nx < 2:
            return pl.ds(0, nx)
        return pl.ds(half * (nx // 2), nx // 2)

    def rows_of(part, half):
        low, size = (split, owner_rows - split) if part else (0, split)
        if half is None or nx >= 2:
            return pl.ds(low, size)
        return pl.ds(low + half * (size // 2), size // 2)

    def item_piece(part, yy, zz, half, kk=None):
        return items.at[k if kk is None else kk, blocks(half), yy, zz, rows_of(part, half)]

    def pass_on(ring, came):
        return [sibling.hand(functools.partial(ring.piece, chunk, half)) for chunk, half in came]

    active = []
    whole = slice(None)

    def start(order, ring, arrived):
        ring.send(1)
        active.append([order, ring, 1, arrived])

    def wave():
        for entry in sorted(active, key=lambda entry: entry[0]):
            _, ring, step, arrived = entry
            if step <= ring.steps():
                came = ring.recv(step)
                ring.send(step + 1)
                arrived(step, came)
                entry[2] += 1

    def second_z(lane):
        def piece(n, half, kk=None):
            kk, size = k if kk is None else kk, nx // LANES
            if half is None:
                return items.at[kk, pl.ds(lane * size, size), :, n, rows_of(0, None)]
            if size > 1:
                return items.at[kk, pl.ds(lane * size + half * (size // 2), size // 2), :, n, rows_of(0, None)]
            return items.at[kk, pl.ds(lane * size, size), :, n, pl.ds(half * (split // 2), split // 2)]

        ring = Ring(net, nz, z, along_z, piece)
        start(1, ring, lambda step, came: pass_on(ring, came))

    def second_y(zz, is_last):
        def arrived(step, came):
            for n, h in came if is_last else []:
                sibling.hand(functools.partial(item_piece, 1, n, whole, h))

        start(2, Ring(net, ny, y, along_y, lambda n, h: item_piece(1, n, zz, h)), arrived)

    def first_y(step, came):
        if step == ay.steps():
            for lane in range(LANES):
                second_z(lane)
            sibling.hand(functools.partial(item_piece, 0, whole, z, None))

    def first_z(step, came):
        for n, chunk in enumerate(came):
            second_y(chunk, step == bz.steps() and n == len(came) - 1)
        if step == bz.steps():
            sibling.hand(functools.partial(item_piece, 1, y, whole, None))

    def couple(chunk, begin):
        @pl.loop(0, row_tiles)
        def _(r):
            pair = jnp.concatenate([users[0, chunk, r], users[1, chunk, r]], axis=1)
            product = jnp.dot(pair, ig[chunk], preferred_element_type=jnp.float32)
            coupled[r] = product if begin else coupled[r] + product

    ay = Direct(net, ny, y, along_y, lambda n, h: item_piece(0, n, z, h))
    bz = Direct(net, nz, z, along_z, lambda n, h: item_piece(1, y, n, h))
    start(0, ay, first_y)
    start(0, bz, first_z)
    second_y(z, bz.steps() == 0)
    if ay.steps() == 0:
        first_y(0, [])
    waves = max(ay.steps() + nz // 2, bz.steps() + ny // 2)
    user_hands = []
    met = xu_step = 0
    for number in range(1, waves + 1):
        wave()
        if number == 1:
            sibling.wait(own_users)
            couple(x, True)
        if number in (2, 4) and xu_step < xu.steps():
            xu_step += 1
            came = xu.recv(xu_step)
            xu.send(xu_step + 1)
            user_hands.append((came, pass_on(xu, came)))
        if number == 3 and user_hands and 2 < nx:
            came, hands = user_hands[0]
            for (chunk, _), hand in zip(came, hands):
                sibling.wait(hand)
                couple(chunk, False)
            met = 1
    while xu_step < xu.steps():
        xu_step += 1
        came = xu.recv(xu_step)
        xu.send(xu_step + 1)
        user_hands.append((came, pass_on(xu, came)))
    for step, (came, hands) in enumerate(user_hands):
        if step >= met:
            for hand in hands:
                sibling.wait(hand)
            for chunk in [came[0][0]] if step == xu.steps() - 1 else [n for n, _ in came]:
                couple(chunk, False)
    sibling.collect()
    own[2].wait()
    to_scalars.wait()

    def panel_block(kk, xx, i):
        panel = meta[2, i]
        return items[kk, xx, lax.div(panel, nz // 2), pl.ds(2 * lax.rem(panel, nz // 2), 2)].reshape(tile, width)

    def product(user_blocks, chunks, i):
        panel = jnp.concatenate([panel_block(kk, xx, i) for xx in chunks for kk in range(2)], axis=1)
        return lax.dot_general(
            jnp.concatenate(user_blocks, axis=1), panel, (((1,), (1,)), ((), ())), preferred_element_type=jnp.float32
        )

    def error_of(prediction, i):
        live = meta[3, i].astype(jnp.float32)
        return (live * (ratings[meta[0, i]].astype(jnp.float32) - prediction)).astype(jnp.bfloat16)

    @pl.loop(0, slots, unroll=UNROLL)
    def _(i):
        row = meta[1, i]
        blocks_of_users = [users[kk, xx, row] for xx in range(nx) for kk in range(2)]
        errors[i] = error_of(product(blocks_of_users, range(nx), i), i)

    running[...] = jnp.zeros_like(running)

    @pl.loop(0, slots, unroll=UNROLL)
    def _(i):
        added = jnp.dot(errors[i], panel_block(k, x, i), preferred_element_type=jnp.float32)
        total = running[...] * meta[4, i].astype(jnp.float32) + added
        running[...] = total
        sums[i] = total

    def newton(factors, gradient, inverse):
        update = jnp.dot(gradient, inverse, precision=HIGHEST, preferred_element_type=jnp.float32)
        return (factors + update).astype(jnp.bfloat16)

    per = row_tiles // PARTS
    rings = []
    own_news = []
    news = [news_0, news_1, news_2, news_3]
    out_copies = []
    for part in range(PARTS):

        @pl.loop(part * per, (part + 1) * per)
        def _(r):
            observed = sums[meta[8, r]] * meta[9, r].astype(jnp.float32)
            factors = users[k, x, r].astype(jnp.float32)
            gradient = observed - UNOBSERVED * coupled[r] - REGULAR * factors
            news[0][k, r] = newton(factors, gradient, ui[...])

        def piece(back, half, kk=None, part=part):
            kk = k if kk is None else kk
            if half is None:
                return news[back].at[kk, pl.ds(part * per, per)]
            return news[back].at[kk, pl.ds(part * per, per), pl.ds(half * (tile // 2), tile // 2)]

        ring = Shift(net, nx, x, along_x, piece)
        ring.send(1)
        own_news.append(sibling.hand(functools.partial(piece, 0, None)))
        rings.append(ring)
        copy = pltpu.make_async_copy(
            news[0].at[k, pl.ds(part * per, per)], unew_out.at[pl.ds(part * per, per)], local_sem.at[3 + part]
        )
        copy.start()
        out_copies.append(copy)
    mine = jnp.concatenate([items[kk, xx, y, z] for xx in range(nx) for kk in range(2)], axis=1)
    icoupled[...] = jnp.dot(mine, ug[...], preferred_element_type=jnp.float32)

    def predict_from(backs, begin, end):
        @pl.loop(0, slots, unroll=UNROLL)
        def _(i):
            row = meta[1, i]
            blocks_of_users = [news[back][kk, row] for back in backs for kk in range(2)]
            value = product(blocks_of_users, [lax.rem(x + back, nx) for back in backs], i)
            value = value if begin else predicted[i] + value
            if end:
                errors[i] = error_of(value, i)
            else:
                predicted[i] = value

    hands = own_news
    for step in range(nx // 2 + 1):
        if step > 0:
            hands = []
            for ring in rings:
                came = ring.recv(step)
                ring.send(step + 1)
                hands += pass_on(ring, came)
        for hand in hands:
            sibling.wait(hand)
        predict_from(sorted({step, (nx - step) % nx}), step == 0, step == nx // 2)

    running[...] = jnp.zeros_like(running)

    @pl.loop(0, slots, unroll=UNROLL)
    def _(i):
        added = lax.dot_general(
            errors[meta[5, i]],
            news[0][k, meta[6, i]],
            (((0,), (0,)), ((), ())),
            preferred_element_type=jnp.float32,
        )
        total = running[...] * meta[7, i].astype(jnp.float32) + added
        running[...] = total
        sums[i] = total

    @pl.loop(0, panels)
    def _(p):
        panel = sums[meta[10, p]] * meta[11, p].astype(jnp.float32)
        pair = panel.astype(jnp.bfloat16).reshape(2, owner_rows, width)
        qs[lax.div(p, nz // 2), pl.ds(2 * lax.rem(p, nz // 2), 2)] = pair

    na = ra.shape[2]
    a_rows, b_rows = pl.ds(0, na), pl.ds(na, owner_rows - na)
    b_slots = [net.slot() for _ in range(1, ny)]
    a_slots = [net.slot() for _ in range(1, nz)]
    for step in range(1, ny):
        to = lax.rem(y + step, ny)
        net.push(b_slots[step - 1], qs.at[to, :, b_rows], rb.at[step - 1], along_y(step))
    for step in range(1, nz):
        to = lax.rem(z + step, nz)
        net.push(a_slots[step - 1], qs.at[:, to, a_rows], ra.at[step - 1], along_z(step))
    for step in range(1, nz):
        net.land(a_slots[step - 1], ra.at[step - 1], along_z(step))
    total = qs[:, z, a_rows].astype(jnp.float32)
    for step in range(1, nz):
        total = total + ra[step - 1].astype(jnp.float32)
    sa[...] = total.astype(jnp.bfloat16)
    c_slots = [net.slot() for _ in range(1, ny)]
    for step in range(1, ny):
        to = lax.rem(y + step, ny)
        net.push(c_slots[step - 1], sa.at[to], ta.at[step - 1], along_y(step))
    for step in range(1, ny):
        net.land(b_slots[step - 1], rb.at[step - 1], along_y(step))
    total = qs[y, :, b_rows].astype(jnp.float32)
    for step in range(1, ny):
        total = total + rb[step - 1].astype(jnp.float32)
    sb[...] = total.astype(jnp.bfloat16)
    d_slots = [net.slot() for _ in range(1, nz)]
    for step in range(1, nz):
        to = lax.rem(z + step, nz)
        net.push(d_slots[step - 1], sb.at[to], tb.at[step - 1], along_z(step))
    for step in range(1, ny):
        net.land(c_slots[step - 1], ta.at[step - 1], along_y(step))
    total_a = sa[y].astype(jnp.float32)
    for step in range(1, ny):
        total_a = total_a + ta[step - 1].astype(jnp.float32)
    for step in range(1, nz):
        net.land(d_slots[step - 1], tb.at[step - 1], along_z(step))
    total_b = sb[z].astype(jnp.float32)
    for step in range(1, nz):
        total_b = total_b + tb[step - 1].astype(jnp.float32)
    observed = jnp.concatenate([total_a, total_b], axis=0)
    factors = items[k, x, y, z].astype(jnp.float32)
    gradient = observed - UNOBSERVED * icoupled[...] - REGULAR * factors
    inew_out[...] = newton(factors, gradient, ii[...])
    for copy in out_copies:
        copy.wait()
    net.drain()


def local(nx, nz, user_factors, item_factors, ratings, tile_coords, tile_count, item_gram, user_gram, user_inverse, item_inverse):
    user_rows, width = user_factors.shape
    owner_rows = item_factors.shape[0]
    slots, tile, _ = ratings.shape
    row_tiles = user_rows // tile
    na = owner_rows * 3 // 8 // 16 * 16
    nb = owner_rows - na
    bf16, f32 = jnp.bfloat16, jnp.float32
    vmem = pl.BlockSpec(memory_space=pltpu.VMEM)
    hbm = pl.BlockSpec(memory_space=pl.ANY)
    user_new, item_new = pl.pallas_call(
        functools.partial(kernel, nx, nz),
        out_shape=(
            jax.ShapeDtypeStruct((row_tiles, tile, width), bf16),
            jax.ShapeDtypeStruct((owner_rows, width), bf16),
        ),
        in_specs=[vmem, pl.BlockSpec(memory_space=pltpu.SMEM), hbm, hbm, hbm, vmem, vmem, vmem, vmem],
        out_specs=(hbm, vmem),
        scratch_shapes=[
            pltpu.VMEM((16, 128), jnp.int32),
            pltpu.SMEM((16, 128), jnp.int32),
            pltpu.VMEM((2, nx, row_tiles, tile, width), bf16),
            pltpu.VMEM((2, nx, NY, nz, owner_rows, width), bf16),
            *[pltpu.VMEM((2, row_tiles, tile, width), bf16)] * 4,
            pltpu.VMEM((slots, tile, tile), bf16),
            pltpu.VMEM((slots, tile, tile), f32),
            pltpu.VMEM((slots, tile, tile), bf16),
            pltpu.VMEM((slots, tile, width), f32),
            pltpu.VMEM((tile, width), f32),
            pltpu.VMEM((row_tiles, tile, width), f32),
            pltpu.VMEM((owner_rows, width), f32),
            pltpu.VMEM((NY, nz, owner_rows, width), bf16),
            pltpu.VMEM((nz - 1, NY, na, width), bf16),
            pltpu.VMEM((NY, na, width), bf16),
            pltpu.VMEM((max(NY - 1, 1), na, width), bf16),
            pltpu.VMEM((max(NY - 1, 1), nz, nb, width), bf16),
            pltpu.VMEM((nz, nb, width), bf16),
            pltpu.VMEM((nz - 1, nb, width), bf16),
            pltpu.SemaphoreType.DMA((SEMS,)),
            pltpu.SemaphoreType.DMA((SEMS,)),
            pltpu.SemaphoreType.DMA((4 + PARTS,)),
        ],
        compiler_params=pltpu.CompilerParams(
            collective_id=0, has_side_effects=True, vmem_limit_bytes=56 * 1024 * 1024
        ),
    )(
        tile_coords.T,
        tile_count,
        user_factors.reshape(row_tiles, tile, width),
        item_factors,
        ratings,
        item_gram.reshape(nx, 2 * width, width),
        user_gram,
        user_inverse,
        item_inverse,
    )
    return user_new.reshape(user_rows, width), item_new


def solution(mesh):
    placed = (
        P("users", "dims"),
        P("users", "dims"),
        P("users", None, None),
        P("users", None),
        P("users"),
        P(None, "dims"),
        P(None, "dims"),
        P("dims", None),
        P("dims", None),
    )
    return jax.shard_map(
        functools.partial(local, mesh.shape["dims"] // 2, mesh.shape["users"] // NY),
        mesh=mesh,
        in_specs=placed,
        out_specs=(P("users", "dims"), P("users", "dims")),
        check_vma=False,
    )
```

```python
import functools

import jax
import jax.numpy as jnp
from jax import lax
from jax.experimental import pallas as pl
from jax.experimental.pallas import tpu as pltpu
from jax.sharding import PartitionSpec as P

UNOBSERVED = 256.0
REGULAR = 2.0
HIGHEST = lax.Precision.HIGHEST
MESH = pl.DeviceIdType.MESH
NY = 4
PARTS = 4
SEMS = 240
UNROLL = 5
LANES = 2


class Net:
    def __init__(self, send_sem, recv_sem):
        self.send_sem = send_sem
        self.recv_sem = recv_sem
        self.used = 0
        self.started = []

    def slot(self):
        self.used += 1
        return self.used - 1

    def push(self, index, source, target, device):
        copy = pltpu.make_async_remote_copy(
            src_ref=source,
            dst_ref=target,
            send_sem=self.send_sem.at[index],
            recv_sem=self.recv_sem.at[index],
            device_id=device,
            device_id_type=MESH,
        )
        copy.start()
        self.started.append(copy)

    def land(self, index, target, device):
        pltpu.make_async_remote_copy(
            src_ref=target,
            dst_ref=target,
            send_sem=self.send_sem.at[index],
            recv_sem=self.recv_sem.at[index],
            device_id=device,
            device_id_type=MESH,
        ).wait_recv()

    def drain(self):
        for copy in self.started:
            copy.wait_send()
        self.started = []


class Ring:
    def __init__(self, net, size, place, to, piece):
        self.net, self.size, self.place, self.to, self.piece = net, size, place, to, piece
        self.slots = {}
        for distance in range(1, size // 2 + 1):
            self.slots[distance] = (net.slot(), net.slot())

    def steps(self):
        return self.size // 2

    def halves(self, distance):
        return (0, 1) if 2 * distance == self.size else (None, None)

    def send(self, distance):
        if distance > self.steps():
            return
        for index, step, half in zip(self.slots[distance], (1, -1), self.halves(distance)):
            chunk = lax.rem(self.place - step * (distance - 1) + self.size, self.size)
            view = self.piece(chunk, half)
            self.net.push(index, view, view, self.to(step))

    def recv(self, distance):
        if distance > self.steps():
            return []
        came = []
        for index, step, half in zip(self.slots[distance], (1, -1), self.halves(distance)):
            chunk = lax.rem(self.place - step * distance + self.size, self.size)
            self.net.land(index, self.piece(chunk, half), self.to(step))
            came.append((chunk, half))
        return came


def cut(size, half):
    return pl.ds(0, size) if half is None else pl.ds(half * (size // 2), size // 2)


class Scatter:
    def __init__(self, net, size, place, to, where, inner, table, landing, relayed, halves):
        self.net, self.size, self.place, self.to, self.where, self.inner = net, size, place, to, where, inner
        self.table, self.landing, self.relayed = table, landing, relayed
        self.far = size // 2 - 1 if size >= 4 and halves else 0
        self.steps = [s for s in range(1, size) if not (self.far and 2 * s == size)]
        self.slots = {s: [net.slot(), net.slot()] for s in self.steps}
        self.passing = [net.slot(), net.slot()]
        self.turn = {0: self.far, 1: size - self.far}

    def chunk(self, step):
        return lax.rem(self.place + step, self.size)

    def push(self, step, half):
        source = self.table.at[self.where(self.chunk(step), half)]
        target = self.landing.at[step - 1] if half is None else self.landing.at[(step - 1, *self.inner(half))]
        self.net.push(self.slots[step][half or 0], source, target, self.to(step))

    def send(self):
        if self.far:
            for half, way in ((0, 1), (1, -1)):
                source = self.table.at[self.where(self.chunk(self.size // 2), half)]
                self.net.push(self.passing[half], source, self.relayed.at[half], self.to(way))
        for step in self.steps:
            if not self.far or step not in self.turn.values():
                self.push(step, None)
        for half in (0, 1) if self.far else ():
            self.push(self.turn[half], 1 - half)

    def relay(self):
        for half, way in ((0, 1), (1, -1)) if self.far else ():
            self.net.land(self.passing[half], self.relayed.at[half], self.to(way))
            place = self.where(self.chunk(self.turn[half]), half)
            value = self.table[place].astype(jnp.float32) + self.relayed[half].astype(jnp.float32)
            self.table[place] = value.astype(jnp.bfloat16)
            self.push(self.turn[half], half)

    def land(self):
        for step in self.steps:
            if not self.far or step not in self.turn.values():
                self.net.land(self.slots[step][0], self.landing.at[step - 1], self.to(step))
            else:
                for half in (0, 1):
                    view = self.landing.at[(step - 1, *self.inner(half))]
                    self.net.land(self.slots[step][half], view, self.to(step))


class Shift(Ring):
    def send(self, distance):
        if distance > self.steps():
            return
        for index, step, half in zip(self.slots[distance], (1, -1), self.halves(distance)):
            here, there = -step * (distance - 1) % self.size, -step * distance % self.size
            self.net.push(index, self.piece(here, half), self.piece(there, half), self.to(step))

    def recv(self, distance):
        came = []
        for index, step, half in zip(self.slots[distance], (1, -1), self.halves(distance)):
            back = -step * distance % self.size
            self.net.land(index, self.piece(back, half), self.to(step))
            came.append((back, half))
        return came


class Direct:
    def __init__(self, net, size, place, to, piece):
        self.net, self.size, self.place, self.to, self.piece = net, size, place, to, piece
        near = [step for step in (1, -1, 2, -2) if abs(step) < size]
        near = [step for n, step in enumerate(near) if step % size not in [e % size for e in near[:n]]]
        self.plan = [[(net.slot(), 0, step, None) for step in near]] if near else []
        if size == 8:
            self.plan.append([(net.slot(), 2, 1, None), (net.slot(), -2, -1, None), (net.slot(), 2, 2, 0), (net.slot(), -2, -2, 1)])

    def steps(self):
        return len(self.plan)

    def chunk(self, back):
        return lax.rem(self.place - back + self.size, self.size)

    def send(self, step):
        if step > self.steps():
            return
        for index, back, jump, half in self.plan[step - 1]:
            view = self.piece(self.chunk(back), half)
            self.net.push(index, view, view, self.to(jump))

    def recv(self, step):
        came = []
        for index, back, jump, half in self.plan[step - 1]:
            chunk = self.chunk(back + jump)
            self.net.land(index, self.piece(chunk, half), self.to(jump))
            if half != 0:
                came.append(chunk)
        return came


class Sibling:
    def __init__(self, net, core, device):
        self.net, self.core, self.device = net, core, device
        self.due = {}

    def hand(self, piece):
        index = self.net.slot()
        view = piece(self.core)
        self.net.push(index, view, view, self.device)
        self.due[index] = piece
        return index

    def wait(self, index):
        self.net.land(index, self.due.pop(index)(1 - self.core), self.device)

    def collect(self):
        for index in list(self.due):
            self.wait(index)


def lookup(coords, count, lines):
    slots = coords.shape[1]
    low = lax.broadcasted_iota(jnp.int32, (slots, slots), 0)
    high = lax.broadcasted_iota(jnp.int32, (slots, slots), 1)

    def down(flat):
        return jnp.sum(jnp.where(low == high, flat, 0), axis=1, keepdims=True)

    def pick(rank, value):
        return jnp.sum(jnp.where(rank == high, value, 0), axis=0, keepdims=True)

    row, panel = coords[0:1, :], coords[1:2, :]
    row_down, panel_down = down(row), down(panel)
    live = (low < count).astype(jnp.int32)

    def rank_of(flat, tall):
        return jnp.sum((flat * slots + high < tall * slots + low).astype(jnp.int32), axis=1, keepdims=True)

    by_row, by_panel = rank_of(row, row_down), rank_of(panel, panel_down)

    def same(rank, value):
        first = lax.broadcasted_iota(jnp.int32, (1, slots), 1) > 0
        return ((pick(rank, value) == pick(rank + 1, value)) & first).astype(jnp.int32)

    def last(value):
        upto = jnp.sum((value <= high).astype(jnp.int32), axis=0, keepdims=True)
        has = jnp.sum((value == high).astype(jnp.int32), axis=0, keepdims=True)
        return jnp.maximum(upto - 1, 0), jnp.minimum(has, 1)

    found = [
        pick(by_row, low),
        pick(by_row, row_down),
        pick(by_row, panel_down),
        pick(by_row, live),
        same(by_row, row_down),
        pick(by_panel, by_row),
        pick(by_panel, row_down),
        same(by_panel, panel_down),
        *last(row_down),
        *last(panel_down),
    ]
    for n, line in enumerate(found):
        lines[n : n + 1, 0:slots] = line


def kernel(
    nx, nz, coords, count, u_hbm, i_hbm, r_hbm, ig, ug, ui, ii, unew_out, inew_out,
    lines, meta, users, items, news_0, news_1, news_2, news_3, ratings, predicted, errors, sums, running, coupled, icoupled,
    qs, ra, sa, ta, rb, sb, tb, yb, za, send_sem, recv_sem, local_sem,
):
    ny = NY
    u = lax.axis_index("users")
    c = lax.axis_index("dims")
    y, z = lax.div(u, nz), lax.rem(u, nz)
    x, k = lax.div(c, 2), lax.rem(c, 2)

    def device(xx, kk, yy, zz):
        return (yy * nz + zz, xx * 2 + kk)

    def along_x(step):
        return device(lax.rem(x + step + nx, nx), k, y, z)

    def along_y(step):
        return device(x, k, lax.rem(y + step + ny, ny), z)

    def along_z(step):
        return device(x, k, y, lax.rem(z + step + nz, nz))

    other_core = device(x, 1 - k, y, z)
    row_tiles, tile, width = users.shape[2:]
    slots = ratings.shape[0]
    panels = ny * nz // 2

    own = [
        pltpu.make_async_copy(i_hbm, items.at[k, x, y, z], local_sem.at[0]),
        pltpu.make_async_copy(u_hbm, users.at[k, x], local_sem.at[1]),
        pltpu.make_async_copy(r_hbm, ratings, local_sem.at[2]),
    ]
    for copy in own:
        copy.start()

    barrier = pltpu.get_barrier_semaphore()
    peers = [along_x(s) for s in range(1, nx)]
    peers += [along_y(s) for s in range(1, ny)]
    peers += [along_z(s) for s in range(1, nz)]
    peers += [other_core]
    for peer in peers:
        pl.semaphore_signal(barrier, inc=1, device_id=peer, device_id_type=MESH)
    lookup(coords, count[0], lines)
    to_scalars = pltpu.make_async_copy(lines, meta, local_sem.at[3 + PARTS])
    to_scalars.start()
    pl.semaphore_wait(barrier, len(peers))

    net = Net(send_sem, recv_sem)
    sibling = Sibling(net, k, other_core)
    own[0].wait()
    own[1].wait()

    first = [net.slot() for _ in range(1, nx)]
    for index, step in zip(first, range(1, nx)):
        view = items.at[k, x, y, z]
        net.push(index, view, view, along_x(step))

    half_rows = row_tiles // 2

    def user_piece(table):
        def piece(chunk, half, kk=None):
            kk = k if kk is None else kk
            if half is None:
                return table.at[kk, chunk]
            return table.at[kk, chunk, pl.ds(half * half_rows, half_rows)]

        return piece

    xu = Ring(net, nx, x, along_x, user_piece(users))
    xu.send(1)
    own_users = sibling.hand(lambda kk: users.at[kk, x])
    for index, step in zip(first, range(1, nx)):
        source = lax.rem(x - step + nx, nx)
        net.land(index, items.at[k, source, y, z], along_x(step))

    owner_rows = items.shape[4]
    split = owner_rows * 3 // 8 // 16 * 16

    def blocks(half):
        if half is None or nx < 2:
            return pl.ds(0, nx)
        return pl.ds(half * (nx // 2), nx // 2)

    def rows_of(part, half):
        low, size = (split, owner_rows - split) if part else (0, split)
        if half is None or nx >= 2:
            return pl.ds(low, size)
        return pl.ds(low + half * (size // 2), size // 2)

    def item_piece(part, yy, zz, half, kk=None):
        return items.at[k if kk is None else kk, blocks(half), yy, zz, rows_of(part, half)]

    def pass_on(ring, came):
        return [sibling.hand(functools.partial(ring.piece, chunk, half)) for chunk, half in came]

    active = []
    whole = slice(None)

    def start(order, ring, arrived):
        ring.send(1)
        active.append([order, ring, 1, arrived])

    def wave():
        for entry in sorted(active, key=lambda entry: entry[0]):
            _, ring, step, arrived = entry
            if step <= ring.steps():
                came = ring.recv(step)
                ring.send(step + 1)
                arrived(step, came)
                entry[2] += 1

    def second_z(lane):
        def piece(n, half, kk=None):
            kk, size = k if kk is None else kk, nx // LANES
            if half is None:
                return items.at[kk, pl.ds(lane * size, size), :, n, rows_of(0, None)]
            if size > 1:
                return items.at[kk, pl.ds(lane * size + half * (size // 2), size // 2), :, n, rows_of(0, None)]
            return items.at[kk, pl.ds(lane * size, size), :, n, pl.ds(half * (split // 2), split // 2)]

        ring = Ring(net, nz, z, along_z, piece)
        start(1, ring, lambda step, came: pass_on(ring, came))

    def second_y(zz, is_last):
        def arrived(step, came):
            for n, h in came if is_last else []:
                sibling.hand(functools.partial(item_piece, 1, n, whole, h))

        start(2, Ring(net, ny, y, along_y, lambda n, h: item_piece(1, n, zz, h)), arrived)

    def first_y(step, came):
        if step == ay.steps():
            for lane in range(LANES):
                second_z(lane)
            sibling.hand(functools.partial(item_piece, 0, whole, z, None))

    def first_z(step, came):
        for n, chunk in enumerate(came):
            second_y(chunk, step == bz.steps() and n == len(came) - 1)
        if step == bz.steps():
            sibling.hand(functools.partial(item_piece, 1, y, whole, None))

    def couple(chunk, begin):
        @pl.loop(0, row_tiles)
        def _(r):
            pair = jnp.concatenate([users[0, chunk, r], users[1, chunk, r]], axis=1)
            product = jnp.dot(pair, ig[chunk], preferred_element_type=jnp.float32)
            coupled[r] = product if begin else coupled[r] + product

    ay = Direct(net, ny, y, along_y, lambda n, h: item_piece(0, n, z, h))
    bz = Direct(net, nz, z, along_z, lambda n, h: item_piece(1, y, n, h))
    start(0, ay, first_y)
    start(0, bz, first_z)
    second_y(z, bz.steps() == 0)
    if ay.steps() == 0:
        first_y(0, [])
    waves = max(ay.steps() + nz // 2, bz.steps() + ny // 2)
    user_hands = []
    met = xu_step = 0
    for number in range(1, waves + 1):
        wave()
        if number == 1:
            sibling.wait(own_users)
            couple(x, True)
        if number in (2, 4) and xu_step < xu.steps():
            xu_step += 1
            came = xu.recv(xu_step)
            xu.send(xu_step + 1)
            user_hands.append((came, pass_on(xu, came)))
        if number == 3 and user_hands and 2 < nx:
            came, hands = user_hands[0]
            for (chunk, _), hand in zip(came, hands):
                sibling.wait(hand)
                couple(chunk, False)
            met = 1
    while xu_step < xu.steps():
        xu_step += 1
        came = xu.recv(xu_step)
        xu.send(xu_step + 1)
        user_hands.append((came, pass_on(xu, came)))
    for step, (came, hands) in enumerate(user_hands):
        if step >= met:
            for hand in hands:
                sibling.wait(hand)
            for chunk in [came[0][0]] if step == xu.steps() - 1 else [n for n, _ in came]:
                couple(chunk, False)
    sibling.collect()
    own[2].wait()
    to_scalars.wait()

    def panel_block(kk, xx, i):
        panel = meta[2, i]
        return items[kk, xx, lax.div(panel, nz // 2), pl.ds(2 * lax.rem(panel, nz // 2), 2)].reshape(tile, width)

    def product(user_blocks, chunks, i):
        panel = jnp.concatenate([panel_block(kk, xx, i) for xx in chunks for kk in range(2)], axis=1)
        return lax.dot_general(
            jnp.concatenate(user_blocks, axis=1), panel, (((1,), (1,)), ((), ())), preferred_element_type=jnp.float32
        )

    def error_of(prediction, i):
        live = meta[3, i].astype(jnp.float32)
        return (live * (ratings[meta[0, i]].astype(jnp.float32) - prediction)).astype(jnp.bfloat16)

    @pl.loop(0, slots, unroll=UNROLL)
    def _(i):
        row = meta[1, i]
        blocks_of_users = [users[kk, xx, row] for xx in range(nx) for kk in range(2)]
        errors[i] = error_of(product(blocks_of_users, range(nx), i), i)

    running[...] = jnp.zeros_like(running)

    @pl.loop(0, slots, unroll=UNROLL)
    def _(i):
        added = jnp.dot(errors[i], panel_block(k, x, i), preferred_element_type=jnp.float32)
        total = running[...] * meta[4, i].astype(jnp.float32) + added
        running[...] = total
        sums[i] = total

    def newton(factors, gradient, inverse):
        update = jnp.dot(gradient, inverse, precision=HIGHEST, preferred_element_type=jnp.float32)
        return (factors + update).astype(jnp.bfloat16)

    per = row_tiles // PARTS
    rings = []
    own_news = []
    news = [news_0, news_1, news_2, news_3]
    out_copies = []
    for part in range(PARTS):

        @pl.loop(part * per, (part + 1) * per)
        def _(r):
            observed = sums[meta[8, r]] * meta[9, r].astype(jnp.float32)
            factors = users[k, x, r].astype(jnp.float32)
            gradient = observed - UNOBSERVED * coupled[r] - REGULAR * factors
            news[0][k, r] = newton(factors, gradient, ui[...])

        def piece(back, half, kk=None, part=part):
            kk = k if kk is None else kk
            if half is None:
                return news[back].at[kk, pl.ds(part * per, per)]
            return news[back].at[kk, pl.ds(part * per, per), pl.ds(half * (tile // 2), tile // 2)]

        ring = Shift(net, nx, x, along_x, piece)
        ring.send(1)
        own_news.append(sibling.hand(functools.partial(piece, 0, None)))
        rings.append(ring)
        copy = pltpu.make_async_copy(
            news[0].at[k, pl.ds(part * per, per)], unew_out.at[pl.ds(part * per, per)], local_sem.at[3 + part]
        )
        copy.start()
        out_copies.append(copy)
    mine = jnp.concatenate([items[kk, xx, y, z] for xx in range(nx) for kk in range(2)], axis=1)
    icoupled[...] = jnp.dot(mine, ug[...], preferred_element_type=jnp.float32)

    def predict_from(backs, begin, end):
        @pl.loop(0, slots, unroll=UNROLL)
        def _(i):
            row = meta[1, i]
            blocks_of_users = [news[back][kk, row] for back in backs for kk in range(2)]
            value = product(blocks_of_users, [lax.rem(x + back, nx) for back in backs], i)
            value = value if begin else predicted[i] + value
            if end:
                errors[i] = error_of(value, i)
            else:
                predicted[i] = value

    hands = own_news
    for step in range(nx // 2 + 1):
        if step > 0:
            hands = []
            for ring in rings:
                came = ring.recv(step)
                ring.send(step + 1)
                hands += pass_on(ring, came)
        for hand in hands:
            sibling.wait(hand)
        predict_from(sorted({step, (nx - step) % nx}), step == 0, step == nx // 2)

    running[...] = jnp.zeros_like(running)

    @pl.loop(0, slots, unroll=UNROLL)
    def _(i):
        added = lax.dot_general(
            errors[meta[5, i]],
            news[0][k, meta[6, i]],
            (((0,), (0,)), ((), ())),
            preferred_element_type=jnp.float32,
        )
        total = running[...] * meta[7, i].astype(jnp.float32) + added
        running[...] = total
        sums[i] = total

    @pl.loop(0, panels)
    def _(p):
        panel = sums[meta[10, p]] * meta[11, p].astype(jnp.float32)
        pair = panel.astype(jnp.bfloat16).reshape(2, owner_rows, width)
        qs[lax.div(p, nz // 2), pl.ds(2 * lax.rem(p, nz // 2), 2)] = pair

    na = ra.shape[2]
    a_rows, b_rows = pl.ds(0, na), pl.ds(na, owner_rows - na)
    b_part = Scatter(net, ny, y, along_y, lambda n, h: (n, cut(nz, h), b_rows), lambda h: (cut(nz, h),), qs, rb, yb, nz > 1)
    a_part = Scatter(net, nz, z, along_z, lambda n, h: (cut(ny, h), n, a_rows), lambda h: (cut(ny, h),), qs, ra, za, ny > 1)
    b_part.send()
    a_part.send()
    b_part.relay()
    a_part.relay()
    a_part.land()
    total = qs[:, z, a_rows].astype(jnp.float32)
    for step in a_part.steps:
        total = total + ra[step - 1].astype(jnp.float32)
    sa[...] = total.astype(jnp.bfloat16)
    c_slots = [net.slot() for _ in range(1, ny)]
    for step in range(1, ny):
        to = lax.rem(y + step, ny)
        net.push(c_slots[step - 1], sa.at[to], ta.at[step - 1], along_y(step))
    b_part.land()
    total = qs[y, :, b_rows].astype(jnp.float32)
    for step in b_part.steps:
        total = total + rb[step - 1].astype(jnp.float32)
    sb[...] = total.astype(jnp.bfloat16)
    d_slots = [net.slot() for _ in range(1, nz)]
    for step in range(1, nz):
        to = lax.rem(z + step, nz)
        net.push(d_slots[step - 1], sb.at[to], tb.at[step - 1], along_z(step))
    for step in range(1, ny):
        net.land(c_slots[step - 1], ta.at[step - 1], along_y(step))
    total_a = sa[y].astype(jnp.float32)
    for step in range(1, ny):
        total_a = total_a + ta[step - 1].astype(jnp.float32)
    for step in range(1, nz):
        net.land(d_slots[step - 1], tb.at[step - 1], along_z(step))
    total_b = sb[z].astype(jnp.float32)
    for step in range(1, nz):
        total_b = total_b + tb[step - 1].astype(jnp.float32)
    observed = jnp.concatenate([total_a, total_b], axis=0)
    factors = items[k, x, y, z].astype(jnp.float32)
    gradient = observed - UNOBSERVED * icoupled[...] - REGULAR * factors
    inew_out[...] = newton(factors, gradient, ii[...])
    for copy in out_copies:
        copy.wait()
    net.drain()


def local(nx, nz, user_factors, item_factors, ratings, tile_coords, tile_count, item_gram, user_gram, user_inverse, item_inverse):
    user_rows, width = user_factors.shape
    owner_rows = item_factors.shape[0]
    slots, tile, _ = ratings.shape
    row_tiles = user_rows // tile
    na = owner_rows // 4
    nb = owner_rows - na
    bf16, f32 = jnp.bfloat16, jnp.float32
    vmem = pl.BlockSpec(memory_space=pltpu.VMEM)
    hbm = pl.BlockSpec(memory_space=pl.ANY)
    user_new, item_new = pl.pallas_call(
        functools.partial(kernel, nx, nz),
        out_shape=(
            jax.ShapeDtypeStruct((row_tiles, tile, width), bf16),
            jax.ShapeDtypeStruct((owner_rows, width), bf16),
        ),
        in_specs=[vmem, pl.BlockSpec(memory_space=pltpu.SMEM), hbm, hbm, hbm, vmem, vmem, vmem, vmem],
        out_specs=(hbm, vmem),
        scratch_shapes=[
            pltpu.VMEM((16, 128), jnp.int32),
            pltpu.SMEM((16, 128), jnp.int32),
            pltpu.VMEM((2, nx, row_tiles, tile, width), bf16),
            pltpu.VMEM((2, nx, NY, nz, owner_rows, width), bf16),
            *[pltpu.VMEM((2, row_tiles, tile, width), bf16)] * 4,
            pltpu.VMEM((slots, tile, tile), bf16),
            pltpu.VMEM((slots, tile, tile), f32),
            pltpu.VMEM((slots, tile, tile), bf16),
            pltpu.VMEM((slots, tile, width), f32),
            pltpu.VMEM((tile, width), f32),
            pltpu.VMEM((row_tiles, tile, width), f32),
            pltpu.VMEM((owner_rows, width), f32),
            pltpu.VMEM((NY, nz, owner_rows, width), bf16),
            pltpu.VMEM((nz - 1, NY, na, width), bf16),
            pltpu.VMEM((NY, na, width), bf16),
            pltpu.VMEM((max(NY - 1, 1), na, width), bf16),
            pltpu.VMEM((max(NY - 1, 1), nz, nb, width), bf16),
            pltpu.VMEM((nz, nb, width), bf16),
            pltpu.VMEM((nz - 1, nb, width), bf16),
            pltpu.VMEM((2, max(nz // 2, 1), nb, width), bf16),
            pltpu.VMEM((2, max(NY // 2, 1), na, width), bf16),
            pltpu.SemaphoreType.DMA((SEMS,)),
            pltpu.SemaphoreType.DMA((SEMS,)),
            pltpu.SemaphoreType.DMA((4 + PARTS,)),
        ],
        compiler_params=pltpu.CompilerParams(
            collective_id=0, has_side_effects=True, vmem_limit_bytes=56 * 1024 * 1024
        ),
    )(
        tile_coords.T,
        tile_count,
        user_factors.reshape(row_tiles, tile, width),
        item_factors,
        ratings,
        item_gram.reshape(nx, 2 * width, width),
        user_gram,
        user_inverse,
        item_inverse,
    )
    return user_new.reshape(user_rows, width), item_new


def solution(mesh):
    placed = (
        P("users", "dims"),
        P("users", "dims"),
        P("users", None, None),
        P("users", None),
        P("users"),
        P(None, "dims"),
        P(None, "dims"),
        P("dims", None),
        P("dims", None),
    )
    return jax.shard_map(
        functools.partial(local, mesh.shape["dims"] // 2, mesh.shape["users"] // NY),
        mesh=mesh,
        in_specs=placed,
        out_specs=(P("users", "dims"), P("users", "dims")),
        check_vma=False,
    )
```

```python
import functools

import jax
import jax.numpy as jnp
from jax import lax
from jax.experimental import pallas as pl
from jax.experimental.pallas import tpu as pltpu
from jax.sharding import PartitionSpec as P

UNOBSERVED = 256.0
REGULAR = 2.0
HIGHEST = lax.Precision.HIGHEST
MESH = pl.DeviceIdType.MESH
NY = 4
PARTS = 4
SEMS = 240
UNROLL = 10
LANES = 2


class Net:
    def __init__(self, send_sem, recv_sem):
        self.send_sem = send_sem
        self.recv_sem = recv_sem
        self.used = 0
        self.started = []

    def slot(self):
        self.used += 1
        return self.used - 1

    def push(self, index, source, target, device):
        copy = pltpu.make_async_remote_copy(
            src_ref=source,
            dst_ref=target,
            send_sem=self.send_sem.at[index],
            recv_sem=self.recv_sem.at[index],
            device_id=device,
            device_id_type=MESH,
        )
        copy.start()
        self.started.append(copy)

    def land(self, index, target, device):
        pltpu.make_async_remote_copy(
            src_ref=target,
            dst_ref=target,
            send_sem=self.send_sem.at[index],
            recv_sem=self.recv_sem.at[index],
            device_id=device,
            device_id_type=MESH,
        ).wait_recv()

    def drain(self):
        for copy in self.started:
            copy.wait_send()
        self.started = []


class Ring:
    def __init__(self, net, size, place, to, piece):
        self.net, self.size, self.place, self.to, self.piece = net, size, place, to, piece
        self.slots = {}
        for distance in range(1, size // 2 + 1):
            self.slots[distance] = (net.slot(), net.slot())

    def steps(self):
        return self.size // 2

    def halves(self, distance):
        return (0, 1) if 2 * distance == self.size else (None, None)

    def send(self, distance):
        if distance > self.steps():
            return
        for index, step, half in zip(self.slots[distance], (1, -1), self.halves(distance)):
            chunk = lax.rem(self.place - step * (distance - 1) + self.size, self.size)
            view = self.piece(chunk, half)
            self.net.push(index, view, view, self.to(step))

    def recv(self, distance):
        if distance > self.steps():
            return []
        came = []
        for index, step, half in zip(self.slots[distance], (1, -1), self.halves(distance)):
            chunk = lax.rem(self.place - step * distance + self.size, self.size)
            self.net.land(index, self.piece(chunk, half), self.to(step))
            came.append((chunk, half))
        return came


def cut(size, half):
    return pl.ds(0, size) if half is None else pl.ds(half * (size // 2), size // 2)


class Scatter:
    def __init__(self, net, size, place, to, where, inner, table, landing, relayed, halves):
        self.net, self.size, self.place, self.to, self.where, self.inner = net, size, place, to, where, inner
        self.table, self.landing, self.relayed = table, landing, relayed
        self.far = size // 2 - 1 if size >= 4 and halves else 0
        self.steps = [s for s in range(1, size) if not (self.far and 2 * s == size)]
        self.slots = {s: [net.slot(), net.slot()] for s in self.steps}
        self.passing = [net.slot(), net.slot()]
        self.turn = {0: self.far, 1: size - self.far}

    def chunk(self, step):
        return lax.rem(self.place + step, self.size)

    def push(self, step, half):
        source = self.table.at[self.where(self.chunk(step), half)]
        target = self.landing.at[step - 1] if half is None else self.landing.at[(step - 1, *self.inner(half))]
        self.net.push(self.slots[step][half or 0], source, target, self.to(step))

    def send(self):
        if self.far:
            for half, way in ((0, 1), (1, -1)):
                source = self.table.at[self.where(self.chunk(self.size // 2), half)]
                self.net.push(self.passing[half], source, self.relayed.at[half], self.to(way))
        for step in self.steps:
            if not self.far or step not in self.turn.values():
                self.push(step, None)
        for half in (0, 1) if self.far else ():
            self.push(self.turn[half], 1 - half)

    def relay(self):
        for half, way in ((0, 1), (1, -1)) if self.far else ():
            self.net.land(self.passing[half], self.relayed.at[half], self.to(way))
            place = self.where(self.chunk(self.turn[half]), half)
            value = self.table[place].astype(jnp.float32) + self.relayed[half].astype(jnp.float32)
            self.table[place] = value.astype(jnp.bfloat16)
            self.push(self.turn[half], half)

    def land(self):
        for step in self.steps:
            if not self.far or step not in self.turn.values():
                self.net.land(self.slots[step][0], self.landing.at[step - 1], self.to(step))
            else:
                for half in (0, 1):
                    view = self.landing.at[(step - 1, *self.inner(half))]
                    self.net.land(self.slots[step][half], view, self.to(step))


class Shift(Ring):
    def send(self, distance):
        if distance > self.steps():
            return
        for index, step, half in zip(self.slots[distance], (1, -1), self.halves(distance)):
            here, there = -step * (distance - 1) % self.size, -step * distance % self.size
            self.net.push(index, self.piece(here, half), self.piece(there, half), self.to(step))

    def recv(self, distance):
        came = []
        for index, step, half in zip(self.slots[distance], (1, -1), self.halves(distance)):
            back = -step * distance % self.size
            self.net.land(index, self.piece(back, half), self.to(step))
            came.append((back, half))
        return came


class Direct:
    def __init__(self, net, size, place, to, piece):
        self.net, self.size, self.place, self.to, self.piece = net, size, place, to, piece
        near = [step for step in (1, -1, 2, -2) if abs(step) < size]
        near = [step for n, step in enumerate(near) if step % size not in [e % size for e in near[:n]]]
        self.plan = [[(net.slot(), 0, step, None) for step in near]] if near else []
        if size == 8:
            self.plan.append([(net.slot(), 2, 1, None), (net.slot(), -2, -1, None), (net.slot(), 2, 2, 0), (net.slot(), -2, -2, 1)])

    def steps(self):
        return len(self.plan)

    def chunk(self, back):
        return lax.rem(self.place - back + self.size, self.size)

    def send(self, step):
        if step > self.steps():
            return
        for index, back, jump, half in self.plan[step - 1]:
            view = self.piece(self.chunk(back), half)
            self.net.push(index, view, view, self.to(jump))

    def recv(self, step):
        came = []
        for index, back, jump, half in self.plan[step - 1]:
            chunk = self.chunk(back + jump)
            self.net.land(index, self.piece(chunk, half), self.to(jump))
            if half != 0:
                came.append(chunk)
        return came


class Sibling:
    def __init__(self, net, core, device):
        self.net, self.core, self.device = net, core, device
        self.due = {}

    def hand(self, piece):
        index = self.net.slot()
        view = piece(self.core)
        self.net.push(index, view, view, self.device)
        self.due[index] = piece
        return index

    def wait(self, index):
        self.net.land(index, self.due.pop(index)(1 - self.core), self.device)

    def collect(self):
        for index in list(self.due):
            self.wait(index)


def lookup(coords, count, lines):
    slots = coords.shape[1]
    low = lax.broadcasted_iota(jnp.int32, (slots, slots), 0)
    high = lax.broadcasted_iota(jnp.int32, (slots, slots), 1)

    def down(flat):
        return jnp.sum(jnp.where(low == high, flat, 0), axis=1, keepdims=True)

    def pick(rank, value):
        return jnp.sum(jnp.where(rank == high, value, 0), axis=0, keepdims=True)

    row, panel = coords[0:1, :], coords[1:2, :]
    row_down, panel_down = down(row), down(panel)
    live = (low < count).astype(jnp.int32)

    def rank_of(flat, tall):
        return jnp.sum((flat * slots + high < tall * slots + low).astype(jnp.int32), axis=1, keepdims=True)

    by_row, by_panel = rank_of(row, row_down), rank_of(panel, panel_down)

    def same(rank, value):
        first = lax.broadcasted_iota(jnp.int32, (1, slots), 1) > 0
        return ((pick(rank, value) == pick(rank + 1, value)) & first).astype(jnp.int32)

    def last(value):
        upto = jnp.sum((value <= high).astype(jnp.int32), axis=0, keepdims=True)
        has = jnp.sum((value == high).astype(jnp.int32), axis=0, keepdims=True)
        return jnp.maximum(upto - 1, 0), jnp.minimum(has, 1)

    found = [
        pick(by_row, low),
        pick(by_row, row_down),
        pick(by_row, panel_down),
        pick(by_row, live),
        same(by_row, row_down),
        pick(by_panel, by_row),
        pick(by_panel, row_down),
        same(by_panel, panel_down),
        *last(row_down),
        *last(panel_down),
    ]
    for n, line in enumerate(found):
        lines[n : n + 1, 0:slots] = line


def kernel(
    nx, nz, coords, count, u_hbm, i_hbm, r_hbm, ig, ug, ui, ii, unew_out, inew_out,
    lines, meta, users, items, news_0, news_1, news_2, news_3, ratings, predicted, errors, sums, running, coupled, icoupled,
    qs, ra, sa, ta, rb, sb, tb, yb, za, send_sem, recv_sem, local_sem,
):
    ny = NY
    u = lax.axis_index("users")
    c = lax.axis_index("dims")
    y, z = lax.div(u, nz), lax.rem(u, nz)
    x, k = lax.div(c, 2), lax.rem(c, 2)

    def device(xx, kk, yy, zz):
        return (yy * nz + zz, xx * 2 + kk)

    def along_x(step):
        return device(lax.rem(x + step + nx, nx), k, y, z)

    def along_y(step):
        return device(x, k, lax.rem(y + step + ny, ny), z)

    def along_z(step):
        return device(x, k, y, lax.rem(z + step + nz, nz))

    other_core = device(x, 1 - k, y, z)
    row_tiles, tile, width = users.shape[2:]
    slots = ratings.shape[0]
    panels = ny * nz // 2

    own = [
        pltpu.make_async_copy(i_hbm, items.at[k, x, y, z], local_sem.at[0]),
        pltpu.make_async_copy(u_hbm, users.at[k, x], local_sem.at[1]),
        pltpu.make_async_copy(r_hbm, ratings, local_sem.at[2]),
    ]
    for copy in own:
        copy.start()

    barrier = pltpu.get_barrier_semaphore()
    peers = [along_x(s) for s in range(1, nx)]
    peers += [along_y(s) for s in range(1, ny)]
    peers += [along_z(s) for s in range(1, nz)]
    peers += [other_core]
    for peer in peers:
        pl.semaphore_signal(barrier, inc=1, device_id=peer, device_id_type=MESH)
    lookup(coords, count[0], lines)
    to_scalars = pltpu.make_async_copy(lines, meta, local_sem.at[3 + PARTS])
    to_scalars.start()
    pl.semaphore_wait(barrier, len(peers))

    net = Net(send_sem, recv_sem)
    sibling = Sibling(net, k, other_core)
    own[0].wait()
    own[1].wait()

    first = [net.slot() for _ in range(1, nx)]
    for index, step in zip(first, range(1, nx)):
        view = items.at[k, x, y, z]
        net.push(index, view, view, along_x(step))

    half_rows = row_tiles // 2

    def user_piece(table):
        def piece(chunk, half, kk=None):
            kk = k if kk is None else kk
            if half is None:
                return table.at[kk, chunk]
            return table.at[kk, chunk, pl.ds(half * half_rows, half_rows)]

        return piece

    xu = Ring(net, nx, x, along_x, user_piece(users))
    xu.send(1)
    own_users = sibling.hand(lambda kk: users.at[kk, x])
    for index, step in zip(first, range(1, nx)):
        source = lax.rem(x - step + nx, nx)
        net.land(index, items.at[k, source, y, z], along_x(step))

    owner_rows = items.shape[4]
    split = owner_rows * 3 // 8 // 16 * 16

    def blocks(half):
        if half is None or nx < 2:
            return pl.ds(0, nx)
        return pl.ds(half * (nx // 2), nx // 2)

    def rows_of(part, half):
        low, size = (split, owner_rows - split) if part else (0, split)
        if half is None or nx >= 2:
            return pl.ds(low, size)
        return pl.ds(low + half * (size // 2), size // 2)

    def item_piece(part, yy, zz, half, kk=None):
        return items.at[k if kk is None else kk, blocks(half), yy, zz, rows_of(part, half)]

    def pass_on(ring, came):
        return [sibling.hand(functools.partial(ring.piece, chunk, half)) for chunk, half in came]

    active = []
    whole = slice(None)

    def start(order, ring, arrived):
        ring.send(1)
        active.append([order, ring, 1, arrived])

    def wave():
        for entry in sorted(active, key=lambda entry: entry[0]):
            _, ring, step, arrived = entry
            if step <= ring.steps():
                came = ring.recv(step)
                ring.send(step + 1)
                arrived(step, came)
                entry[2] += 1

    def second_z(lane):
        def piece(n, half, kk=None):
            kk, size = k if kk is None else kk, nx // LANES
            if half is None:
                return items.at[kk, pl.ds(lane * size, size), :, n, rows_of(0, None)]
            if size > 1:
                return items.at[kk, pl.ds(lane * size + half * (size // 2), size // 2), :, n, rows_of(0, None)]
            return items.at[kk, pl.ds(lane * size, size), :, n, pl.ds(half * (split // 2), split // 2)]

        ring = Ring(net, nz, z, along_z, piece)
        start(1, ring, lambda step, came: pass_on(ring, came))

    def second_y(zz, is_last):
        def arrived(step, came):
            for n, h in came if is_last else []:
                sibling.hand(functools.partial(item_piece, 1, n, whole, h))

        start(2, Ring(net, ny, y, along_y, lambda n, h: item_piece(1, n, zz, h)), arrived)

    def first_y(step, came):
        if step == ay.steps():
            for lane in range(LANES):
                second_z(lane)
            sibling.hand(functools.partial(item_piece, 0, whole, z, None))

    def first_z(step, came):
        for n, chunk in enumerate(came):
            second_y(chunk, step == bz.steps() and n == len(came) - 1)
        if step == bz.steps():
            sibling.hand(functools.partial(item_piece, 1, y, whole, None))

    def couple(chunk, begin):
        @pl.loop(0, row_tiles)
        def _(r):
            pair = jnp.concatenate([users[0, chunk, r], users[1, chunk, r]], axis=1)
            product = jnp.dot(pair, ig[chunk], preferred_element_type=jnp.float32)
            coupled[r] = product if begin else coupled[r] + product

    ay = Direct(net, ny, y, along_y, lambda n, h: item_piece(0, n, z, h))
    bz = Direct(net, nz, z, along_z, lambda n, h: item_piece(1, y, n, h))
    start(0, ay, first_y)
    start(0, bz, first_z)
    second_y(z, bz.steps() == 0)
    if ay.steps() == 0:
        first_y(0, [])
    waves = max(ay.steps() + nz // 2, bz.steps() + ny // 2)
    user_hands = []
    met = xu_step = 0
    for number in range(1, waves + 1):
        wave()
        if number == 1:
            sibling.wait(own_users)
            couple(x, True)
        if number in (2, 4) and xu_step < xu.steps():
            xu_step += 1
            came = xu.recv(xu_step)
            xu.send(xu_step + 1)
            user_hands.append((came, pass_on(xu, came)))
        if number == 3 and user_hands and 2 < nx:
            came, hands = user_hands[0]
            for (chunk, _), hand in zip(came, hands):
                sibling.wait(hand)
                couple(chunk, False)
            met = 1
    while xu_step < xu.steps():
        xu_step += 1
        came = xu.recv(xu_step)
        xu.send(xu_step + 1)
        user_hands.append((came, pass_on(xu, came)))
    for step, (came, hands) in enumerate(user_hands):
        if step >= met:
            for hand in hands:
                sibling.wait(hand)
            for chunk in [came[0][0]] if step == xu.steps() - 1 else [n for n, _ in came]:
                couple(chunk, False)
    sibling.collect()
    own[2].wait()
    to_scalars.wait()

    def panel_block(kk, xx, i):
        panel = meta[2, i]
        return items[kk, xx, lax.div(panel, nz // 2), pl.ds(2 * lax.rem(panel, nz // 2), 2)].reshape(tile, width)

    def product(user_blocks, chunks, i):
        panel = jnp.concatenate([panel_block(kk, xx, i) for xx in chunks for kk in range(2)], axis=1)
        return lax.dot_general(
            jnp.concatenate(user_blocks, axis=1), panel, (((1,), (1,)), ((), ())), preferred_element_type=jnp.float32
        )

    def error_of(prediction, i):
        live = meta[3, i].astype(jnp.float32)
        return (live * (ratings[meta[0, i]].astype(jnp.float32) - prediction)).astype(jnp.bfloat16)

    @pl.loop(0, slots, unroll=UNROLL)
    def _(i):
        row = meta[1, i]
        blocks_of_users = [users[kk, xx, row] for xx in range(nx) for kk in range(2)]
        errors[i] = error_of(product(blocks_of_users, range(nx), i), i)

    running[...] = jnp.zeros_like(running)

    @pl.loop(0, slots, unroll=UNROLL)
    def _(i):
        added = jnp.dot(errors[i], panel_block(k, x, i), preferred_element_type=jnp.float32)
        total = running[...] * meta[4, i].astype(jnp.float32) + added
        running[...] = total
        sums[i] = total

    def newton(factors, gradient, inverse):
        update = jnp.dot(gradient, inverse, precision=HIGHEST, preferred_element_type=jnp.float32)
        return (factors + update).astype(jnp.bfloat16)

    per = row_tiles // PARTS
    rings = []
    own_news = []
    news = [news_0, news_1, news_2, news_3]
    out_copies = []
    for part in range(PARTS):

        @pl.loop(part * per, (part + 1) * per)
        def _(r):
            observed = sums[meta[8, r]] * meta[9, r].astype(jnp.float32)
            factors = users[k, x, r].astype(jnp.float32)
            gradient = observed - UNOBSERVED * coupled[r] - REGULAR * factors
            news[0][k, r] = newton(factors, gradient, ui[...])

        def piece(back, half, kk=None, part=part):
            kk = k if kk is None else kk
            if half is None:
                return news[back].at[kk, pl.ds(part * per, per)]
            return news[back].at[kk, pl.ds(part * per, per), pl.ds(half * (tile // 2), tile // 2)]

        ring = Shift(net, nx, x, along_x, piece)
        ring.send(1)
        own_news.append(sibling.hand(functools.partial(piece, 0, None)))
        rings.append(ring)
        copy = pltpu.make_async_copy(
            news[0].at[k, pl.ds(part * per, per)], unew_out.at[pl.ds(part * per, per)], local_sem.at[3 + part]
        )
        copy.start()
        out_copies.append(copy)
    mine = jnp.concatenate([items[kk, xx, y, z] for xx in range(nx) for kk in range(2)], axis=1)
    icoupled[...] = jnp.dot(mine, ug[...], preferred_element_type=jnp.float32)

    def predict_from(backs, begin, end):
        @pl.loop(0, slots, unroll=UNROLL)
        def _(i):
            row = meta[1, i]
            blocks_of_users = [news[back][kk, row] for back in backs for kk in range(2)]
            value = product(blocks_of_users, [lax.rem(x + back, nx) for back in backs], i)
            value = value if begin else predicted[i] + value
            if end:
                errors[i] = error_of(value, i)
            else:
                predicted[i] = value

    hands = own_news
    for step in range(nx // 2 + 1):
        if step > 0:
            hands = []
            for ring in rings:
                came = ring.recv(step)
                ring.send(step + 1)
                hands += pass_on(ring, came)
        for hand in hands:
            sibling.wait(hand)
        predict_from(sorted({step, (nx - step) % nx}), step == 0, step == nx // 2)

    running[...] = jnp.zeros_like(running)

    @pl.loop(0, slots, unroll=UNROLL)
    def _(i):
        added = lax.dot_general(
            errors[meta[5, i]],
            news[0][k, meta[6, i]],
            (((0,), (0,)), ((), ())),
            preferred_element_type=jnp.float32,
        )
        total = running[...] * meta[7, i].astype(jnp.float32) + added
        running[...] = total
        sums[i] = total

    @pl.loop(0, panels)
    def _(p):
        panel = sums[meta[10, p]] * meta[11, p].astype(jnp.float32)
        pair = panel.astype(jnp.bfloat16).reshape(2, owner_rows, width)
        qs[lax.div(p, nz // 2), pl.ds(2 * lax.rem(p, nz // 2), 2)] = pair

    na = ra.shape[2]
    a_rows, b_rows = pl.ds(0, na), pl.ds(na, owner_rows - na)
    b_part = Scatter(net, ny, y, along_y, lambda n, h: (n, cut(nz, h), b_rows), lambda h: (cut(nz, h),), qs, rb, yb, nz > 1)
    a_part = Scatter(net, nz, z, along_z, lambda n, h: (cut(ny, h), n, a_rows), lambda h: (cut(ny, h),), qs, ra, za, ny > 1)
    b_part.send()
    a_part.send()
    b_part.relay()
    a_part.relay()
    a_part.land()
    total = qs[:, z, a_rows].astype(jnp.float32)
    for step in a_part.steps:
        total = total + ra[step - 1].astype(jnp.float32)
    sa[...] = total.astype(jnp.bfloat16)
    c_slots = [net.slot() for _ in range(1, ny)]
    for step in range(1, ny):
        to = lax.rem(y + step, ny)
        net.push(c_slots[step - 1], sa.at[to], ta.at[step - 1], along_y(step))
    b_part.land()
    total = qs[y, :, b_rows].astype(jnp.float32)
    for step in b_part.steps:
        total = total + rb[step - 1].astype(jnp.float32)
    sb[...] = total.astype(jnp.bfloat16)
    d_slots = [net.slot() for _ in range(1, nz)]
    for step in range(1, nz):
        to = lax.rem(z + step, nz)
        net.push(d_slots[step - 1], sb.at[to], tb.at[step - 1], along_z(step))
    for step in range(1, ny):
        net.land(c_slots[step - 1], ta.at[step - 1], along_y(step))
    total_a = sa[y].astype(jnp.float32)
    for step in range(1, ny):
        total_a = total_a + ta[step - 1].astype(jnp.float32)
    for step in range(1, nz):
        net.land(d_slots[step - 1], tb.at[step - 1], along_z(step))
    total_b = sb[z].astype(jnp.float32)
    for step in range(1, nz):
        total_b = total_b + tb[step - 1].astype(jnp.float32)
    observed = jnp.concatenate([total_a, total_b], axis=0)
    factors = items[k, x, y, z].astype(jnp.float32)
    gradient = observed - UNOBSERVED * icoupled[...] - REGULAR * factors
    inew_out[...] = newton(factors, gradient, ii[...])
    for copy in out_copies:
        copy.wait()
    net.drain()


def local(nx, nz, user_factors, item_factors, ratings, tile_coords, tile_count, item_gram, user_gram, user_inverse, item_inverse):
    user_rows, width = user_factors.shape
    owner_rows = item_factors.shape[0]
    slots, tile, _ = ratings.shape
    row_tiles = user_rows // tile
    na = owner_rows // 4
    nb = owner_rows - na
    bf16, f32 = jnp.bfloat16, jnp.float32
    vmem = pl.BlockSpec(memory_space=pltpu.VMEM)
    hbm = pl.BlockSpec(memory_space=pl.ANY)
    user_new, item_new = pl.pallas_call(
        functools.partial(kernel, nx, nz),
        out_shape=(
            jax.ShapeDtypeStruct((row_tiles, tile, width), bf16),
            jax.ShapeDtypeStruct((owner_rows, width), bf16),
        ),
        in_specs=[vmem, pl.BlockSpec(memory_space=pltpu.SMEM), hbm, hbm, hbm, vmem, vmem, vmem, vmem],
        out_specs=(hbm, vmem),
        scratch_shapes=[
            pltpu.VMEM((16, 128), jnp.int32),
            pltpu.SMEM((16, 128), jnp.int32),
            pltpu.VMEM((2, nx, row_tiles, tile, width), bf16),
            pltpu.VMEM((2, nx, NY, nz, owner_rows, width), bf16),
            *[pltpu.VMEM((2, row_tiles, tile, width), bf16)] * 4,
            pltpu.VMEM((slots, tile, tile), bf16),
            pltpu.VMEM((slots, tile, tile), f32),
            pltpu.VMEM((slots, tile, tile), bf16),
            pltpu.VMEM((slots, tile, width), f32),
            pltpu.VMEM((tile, width), f32),
            pltpu.VMEM((row_tiles, tile, width), f32),
            pltpu.VMEM((owner_rows, width), f32),
            pltpu.VMEM((NY, nz, owner_rows, width), bf16),
            pltpu.VMEM((nz - 1, NY, na, width), bf16),
            pltpu.VMEM((NY, na, width), bf16),
            pltpu.VMEM((max(NY - 1, 1), na, width), bf16),
            pltpu.VMEM((max(NY - 1, 1), nz, nb, width), bf16),
            pltpu.VMEM((nz, nb, width), bf16),
            pltpu.VMEM((nz - 1, nb, width), bf16),
            pltpu.VMEM((2, max(nz // 2, 1), nb, width), bf16),
            pltpu.VMEM((2, max(NY // 2, 1), na, width), bf16),
            pltpu.SemaphoreType.DMA((SEMS,)),
            pltpu.SemaphoreType.DMA((SEMS,)),
            pltpu.SemaphoreType.DMA((4 + PARTS,)),
        ],
        compiler_params=pltpu.CompilerParams(
            collective_id=0, has_side_effects=True, vmem_limit_bytes=56 * 1024 * 1024
        ),
    )(
        tile_coords.T,
        tile_count,
        user_factors.reshape(row_tiles, tile, width),
        item_factors,
        ratings,
        item_gram.reshape(nx, 2 * width, width),
        user_gram,
        user_inverse,
        item_inverse,
    )
    return user_new.reshape(user_rows, width), item_new


def solution(mesh):
    placed = (
        P("users", "dims"),
        P("users", "dims"),
        P("users", None, None),
        P("users", None),
        P("users"),
        P(None, "dims"),
        P(None, "dims"),
        P("dims", None),
        P("dims", None),
    )
    return jax.shard_map(
        functools.partial(local, mesh.shape["dims"] // 2, mesh.shape["users"] // NY),
        mesh=mesh,
        in_specs=placed,
        out_specs=(P("users", "dims"), P("users", "dims")),
        check_vma=False,
    )
```

```python
import functools

import jax
import jax.numpy as jnp
from jax import lax
from jax.experimental import pallas as pl
from jax.experimental.pallas import tpu as pltpu
from jax.sharding import PartitionSpec as P

UNOBSERVED = 256.0
REGULAR = 2.0
HIGHEST = lax.Precision.HIGHEST
MESH = pl.DeviceIdType.MESH
NY = 4
PARTS = 4
SEMS = 240
UNROLL = 15
LANES = 2


class Net:
    def __init__(self, send_sem, recv_sem):
        self.send_sem = send_sem
        self.recv_sem = recv_sem
        self.used = 0
        self.started = []

    def slot(self):
        self.used += 1
        return self.used - 1

    def push(self, index, source, target, device):
        copy = pltpu.make_async_remote_copy(
            src_ref=source,
            dst_ref=target,
            send_sem=self.send_sem.at[index],
            recv_sem=self.recv_sem.at[index],
            device_id=device,
            device_id_type=MESH,
        )
        copy.start()
        self.started.append(copy)

    def land(self, index, target, device):
        pltpu.make_async_remote_copy(
            src_ref=target,
            dst_ref=target,
            send_sem=self.send_sem.at[index],
            recv_sem=self.recv_sem.at[index],
            device_id=device,
            device_id_type=MESH,
        ).wait_recv()

    def drain(self):
        for copy in self.started:
            copy.wait_send()
        self.started = []


class Ring:
    def __init__(self, net, size, place, to, piece):
        self.net, self.size, self.place, self.to, self.piece = net, size, place, to, piece
        self.slots = {}
        for distance in range(1, size // 2 + 1):
            self.slots[distance] = (net.slot(), net.slot())

    def steps(self):
        return self.size // 2

    def halves(self, distance):
        return (0, 1) if 2 * distance == self.size else (None, None)

    def send(self, distance):
        if distance > self.steps():
            return
        for index, step, half in zip(self.slots[distance], (1, -1), self.halves(distance)):
            chunk = lax.rem(self.place - step * (distance - 1) + self.size, self.size)
            view = self.piece(chunk, half)
            self.net.push(index, view, view, self.to(step))

    def recv(self, distance):
        if distance > self.steps():
            return []
        came = []
        for index, step, half in zip(self.slots[distance], (1, -1), self.halves(distance)):
            chunk = lax.rem(self.place - step * distance + self.size, self.size)
            self.net.land(index, self.piece(chunk, half), self.to(step))
            came.append((chunk, half))
        return came


def cut(size, half):
    return pl.ds(0, size) if half is None else pl.ds(half * (size // 2), size // 2)


class Scatter:
    def __init__(self, net, size, place, to, where, inner, table, landing, relayed, halves):
        self.net, self.size, self.place, self.to, self.where, self.inner = net, size, place, to, where, inner
        self.table, self.landing, self.relayed = table, landing, relayed
        self.far = size // 2 - 1 if size >= 4 and halves else 0
        self.steps = [s for s in range(1, size) if not (self.far and 2 * s == size)]
        self.slots = {s: [net.slot(), net.slot()] for s in self.steps}
        self.passing = [net.slot(), net.slot()]
        self.turn = {0: self.far, 1: size - self.far}

    def chunk(self, step):
        return lax.rem(self.place + step, self.size)

    def push(self, step, half):
        source = self.table.at[self.where(self.chunk(step), half)]
        target = self.landing.at[step - 1] if half is None else self.landing.at[(step - 1, *self.inner(half))]
        self.net.push(self.slots[step][half or 0], source, target, self.to(step))

    def send(self):
        if self.far:
            for half, way in ((0, 1), (1, -1)):
                source = self.table.at[self.where(self.chunk(self.size // 2), half)]
                self.net.push(self.passing[half], source, self.relayed.at[half], self.to(way))
        for step in self.steps:
            if not self.far or step not in self.turn.values():
                self.push(step, None)
        for half in (0, 1) if self.far else ():
            self.push(self.turn[half], 1 - half)

    def relay(self):
        for half, way in ((0, 1), (1, -1)) if self.far else ():
            self.net.land(self.passing[half], self.relayed.at[half], self.to(way))
            place = self.where(self.chunk(self.turn[half]), half)
            value = self.table[place].astype(jnp.float32) + self.relayed[half].astype(jnp.float32)
            self.table[place] = value.astype(jnp.bfloat16)
            self.push(self.turn[half], half)

    def land(self):
        for step in self.steps:
            if not self.far or step not in self.turn.values():
                self.net.land(self.slots[step][0], self.landing.at[step - 1], self.to(step))
            else:
                for half in (0, 1):
                    view = self.landing.at[(step - 1, *self.inner(half))]
                    self.net.land(self.slots[step][half], view, self.to(step))


class Shift(Ring):
    def send(self, distance):
        if distance > self.steps():
            return
        for index, step, half in zip(self.slots[distance], (1, -1), self.halves(distance)):
            here, there = -step * (distance - 1) % self.size, -step * distance % self.size
            self.net.push(index, self.piece(here, half), self.piece(there, half), self.to(step))

    def recv(self, distance):
        came = []
        for index, step, half in zip(self.slots[distance], (1, -1), self.halves(distance)):
            back = -step * distance % self.size
            self.net.land(index, self.piece(back, half), self.to(step))
            came.append((back, half))
        return came


class Direct:
    def __init__(self, net, size, place, to, piece):
        self.net, self.size, self.place, self.to, self.piece = net, size, place, to, piece
        near = [step for step in (1, -1, 2, -2) if abs(step) < size]
        near = [step for n, step in enumerate(near) if step % size not in [e % size for e in near[:n]]]
        self.plan = [[(net.slot(), 0, step, None) for step in near]] if near else []
        if size == 8:
            self.plan.append([(net.slot(), 2, 1, None), (net.slot(), -2, -1, None), (net.slot(), 2, 2, 0), (net.slot(), -2, -2, 1)])

    def steps(self):
        return len(self.plan)

    def chunk(self, back):
        return lax.rem(self.place - back + self.size, self.size)

    def send(self, step):
        if step > self.steps():
            return
        for index, back, jump, half in self.plan[step - 1]:
            view = self.piece(self.chunk(back), half)
            self.net.push(index, view, view, self.to(jump))

    def recv(self, step):
        came = []
        for index, back, jump, half in self.plan[step - 1]:
            chunk = self.chunk(back + jump)
            self.net.land(index, self.piece(chunk, half), self.to(jump))
            if half != 0:
                came.append(chunk)
        return came


class Sibling:
    def __init__(self, net, core, device):
        self.net, self.core, self.device = net, core, device
        self.due = {}

    def hand(self, piece):
        index = self.net.slot()
        view = piece(self.core)
        self.net.push(index, view, view, self.device)
        self.due[index] = piece
        return index

    def wait(self, index):
        self.net.land(index, self.due.pop(index)(1 - self.core), self.device)

    def collect(self):
        for index in list(self.due):
            self.wait(index)


def lookup(coords, count, lines):
    slots = coords.shape[1]
    low = lax.broadcasted_iota(jnp.int32, (slots, slots), 0)
    high = lax.broadcasted_iota(jnp.int32, (slots, slots), 1)

    def down(flat):
        return jnp.sum(jnp.where(low == high, flat, 0), axis=1, keepdims=True)

    def pick(rank, value):
        return jnp.sum(jnp.where(rank == high, value, 0), axis=0, keepdims=True)

    row, panel = coords[0:1, :], coords[1:2, :]
    row_down, panel_down = down(row), down(panel)
    live = (low < count).astype(jnp.int32)

    def rank_of(flat, tall):
        return jnp.sum((flat * slots + high < tall * slots + low).astype(jnp.int32), axis=1, keepdims=True)

    by_row, by_panel = rank_of(row, row_down), rank_of(panel, panel_down)

    def same(rank, value):
        first = lax.broadcasted_iota(jnp.int32, (1, slots), 1) > 0
        return ((pick(rank, value) == pick(rank + 1, value)) & first).astype(jnp.int32)

    def last(value):
        upto = jnp.sum((value <= high).astype(jnp.int32), axis=0, keepdims=True)
        has = jnp.sum((value == high).astype(jnp.int32), axis=0, keepdims=True)
        return jnp.maximum(upto - 1, 0), jnp.minimum(has, 1)

    found = [
        pick(by_row, low),
        pick(by_row, row_down),
        pick(by_row, panel_down),
        pick(by_row, live),
        same(by_row, row_down),
        pick(by_panel, by_row),
        pick(by_panel, row_down),
        same(by_panel, panel_down),
        *last(row_down),
        *last(panel_down),
    ]
    for n, line in enumerate(found):
        lines[n : n + 1, 0:slots] = line


def kernel(
    nx, nz, coords, count, u_hbm, i_hbm, r_hbm, ig, ug, ui, ii, unew_out, inew_out,
    lines, meta, users, items, news_0, news_1, news_2, news_3, ratings, predicted, errors, sums, running, coupled, icoupled,
    qs, ra, sa, ta, rb, sb, tb, yb, za, send_sem, recv_sem, local_sem,
):
    ny = NY
    u = lax.axis_index("users")
    c = lax.axis_index("dims")
    y, z = lax.div(u, nz), lax.rem(u, nz)
    x, k = lax.div(c, 2), lax.rem(c, 2)

    def device(xx, kk, yy, zz):
        return (yy * nz + zz, xx * 2 + kk)

    def along_x(step):
        return device(lax.rem(x + step + nx, nx), k, y, z)

    def along_y(step):
        return device(x, k, lax.rem(y + step + ny, ny), z)

    def along_z(step):
        return device(x, k, y, lax.rem(z + step + nz, nz))

    other_core = device(x, 1 - k, y, z)
    row_tiles, tile, width = users.shape[2:]
    slots = ratings.shape[0]
    panels = ny * nz // 2

    own = [
        pltpu.make_async_copy(i_hbm, items.at[k, x, y, z], local_sem.at[0]),
        pltpu.make_async_copy(u_hbm, users.at[k, x], local_sem.at[1]),
        pltpu.make_async_copy(r_hbm, ratings, local_sem.at[2]),
    ]
    for copy in own:
        copy.start()

    barrier = pltpu.get_barrier_semaphore()
    peers = [along_x(s) for s in range(1, nx)]
    peers += [along_y(s) for s in range(1, ny)]
    peers += [along_z(s) for s in range(1, nz)]
    peers += [other_core]
    for peer in peers:
        pl.semaphore_signal(barrier, inc=1, device_id=peer, device_id_type=MESH)
    lookup(coords, count[0], lines)
    to_scalars = pltpu.make_async_copy(lines, meta, local_sem.at[3 + PARTS])
    to_scalars.start()
    pl.semaphore_wait(barrier, len(peers))

    net = Net(send_sem, recv_sem)
    sibling = Sibling(net, k, other_core)
    own[0].wait()
    own[1].wait()

    first = [net.slot() for _ in range(1, nx)]
    for index, step in zip(first, range(1, nx)):
        view = items.at[k, x, y, z]
        net.push(index, view, view, along_x(step))

    half_rows = row_tiles // 2

    def user_piece(table):
        def piece(chunk, half, kk=None):
            kk = k if kk is None else kk
            if half is None:
                return table.at[kk, chunk]
            return table.at[kk, chunk, pl.ds(half * half_rows, half_rows)]

        return piece

    xu = Ring(net, nx, x, along_x, user_piece(users))
    xu.send(1)
    own_users = sibling.hand(lambda kk: users.at[kk, x])
    for index, step in zip(first, range(1, nx)):
        source = lax.rem(x - step + nx, nx)
        net.land(index, items.at[k, source, y, z], along_x(step))

    owner_rows = items.shape[4]
    split = owner_rows * 3 // 8 // 16 * 16

    def blocks(half):
        if half is None or nx < 2:
            return pl.ds(0, nx)
        return pl.ds(half * (nx // 2), nx // 2)

    def rows_of(part, half):
        low, size = (split, owner_rows - split) if part else (0, split)
        if half is None or nx >= 2:
            return pl.ds(low, size)
        return pl.ds(low + half * (size // 2), size // 2)

    def item_piece(part, yy, zz, half, kk=None):
        return items.at[k if kk is None else kk, blocks(half), yy, zz, rows_of(part, half)]

    def pass_on(ring, came):
        return [sibling.hand(functools.partial(ring.piece, chunk, half)) for chunk, half in came]

    active = []
    whole = slice(None)

    def start(order, ring, arrived):
        ring.send(1)
        active.append([order, ring, 1, arrived])

    def wave():
        for entry in sorted(active, key=lambda entry: entry[0]):
            _, ring, step, arrived = entry
            if step <= ring.steps():
                came = ring.recv(step)
                ring.send(step + 1)
                arrived(step, came)
                entry[2] += 1

    def second_z(lane):
        def piece(n, half, kk=None):
            kk, size = k if kk is None else kk, nx // LANES
            if half is None:
                return items.at[kk, pl.ds(lane * size, size), :, n, rows_of(0, None)]
            if size > 1:
                return items.at[kk, pl.ds(lane * size + half * (size // 2), size // 2), :, n, rows_of(0, None)]
            return items.at[kk, pl.ds(lane * size, size), :, n, pl.ds(half * (split // 2), split // 2)]

        ring = Ring(net, nz, z, along_z, piece)
        start(1, ring, lambda step, came: pass_on(ring, came))

    def second_y(zz, is_last):
        def arrived(step, came):
            for n, h in came if is_last else []:
                sibling.hand(functools.partial(item_piece, 1, n, whole, h))

        start(2, Ring(net, ny, y, along_y, lambda n, h: item_piece(1, n, zz, h)), arrived)

    def first_y(step, came):
        if step == ay.steps():
            for lane in range(LANES):
                second_z(lane)
            sibling.hand(functools.partial(item_piece, 0, whole, z, None))

    def first_z(step, came):
        for n, chunk in enumerate(came):
            second_y(chunk, step == bz.steps() and n == len(came) - 1)
        if step == bz.steps():
            sibling.hand(functools.partial(item_piece, 1, y, whole, None))

    def couple(chunk, begin):
        @pl.loop(0, row_tiles)
        def _(r):
            pair = jnp.concatenate([users[0, chunk, r], users[1, chunk, r]], axis=1)
            product = jnp.dot(pair, ig[chunk], preferred_element_type=jnp.float32)
            coupled[r] = product if begin else coupled[r] + product

    ay = Direct(net, ny, y, along_y, lambda n, h: item_piece(0, n, z, h))
    bz = Direct(net, nz, z, along_z, lambda n, h: item_piece(1, y, n, h))
    start(0, ay, first_y)
    start(0, bz, first_z)
    second_y(z, bz.steps() == 0)
    if ay.steps() == 0:
        first_y(0, [])
    waves = max(ay.steps() + nz // 2, bz.steps() + ny // 2)
    user_hands = []
    met = xu_step = 0
    for number in range(1, waves + 1):
        wave()
        if number == 1:
            sibling.wait(own_users)
            couple(x, True)
        if number in (2, 4) and xu_step < xu.steps():
            xu_step += 1
            came = xu.recv(xu_step)
            xu.send(xu_step + 1)
            user_hands.append((came, pass_on(xu, came)))
        if number == 3 and user_hands and 2 < nx:
            came, hands = user_hands[0]
            for (chunk, _), hand in zip(came, hands):
                sibling.wait(hand)
                couple(chunk, False)
            met = 1
    while xu_step < xu.steps():
        xu_step += 1
        came = xu.recv(xu_step)
        xu.send(xu_step + 1)
        user_hands.append((came, pass_on(xu, came)))
    for step, (came, hands) in enumerate(user_hands):
        if step >= met:
            for hand in hands:
                sibling.wait(hand)
            for chunk in [came[0][0]] if step == xu.steps() - 1 else [n for n, _ in came]:
                couple(chunk, False)
    sibling.collect()
    own[2].wait()
    to_scalars.wait()

    def panel_block(kk, xx, i):
        panel = meta[2, i]
        return items[kk, xx, lax.div(panel, nz // 2), pl.ds(2 * lax.rem(panel, nz // 2), 2)].reshape(tile, width)

    def product(user_blocks, chunks, i):
        panel = jnp.concatenate([panel_block(kk, xx, i) for xx in chunks for kk in range(2)], axis=1)
        return lax.dot_general(
            jnp.concatenate(user_blocks, axis=1), panel, (((1,), (1,)), ((), ())), preferred_element_type=jnp.float32
        )

    def error_of(prediction, i):
        live = meta[3, i].astype(jnp.float32)
        return (live * (ratings[meta[0, i]].astype(jnp.float32) - prediction)).astype(jnp.bfloat16)

    @pl.loop(0, slots, unroll=UNROLL)
    def _(i):
        row = meta[1, i]
        blocks_of_users = [users[kk, xx, row] for xx in range(nx) for kk in range(2)]
        errors[i] = error_of(product(blocks_of_users, range(nx), i), i)

    running[...] = jnp.zeros_like(running)

    @pl.loop(0, slots, unroll=UNROLL)
    def _(i):
        added = jnp.dot(errors[i], panel_block(k, x, i), preferred_element_type=jnp.float32)
        total = running[...] * meta[4, i].astype(jnp.float32) + added
        running[...] = total
        sums[i] = total

    def newton(factors, gradient, inverse):
        update = jnp.dot(gradient, inverse, precision=HIGHEST, preferred_element_type=jnp.float32)
        return (factors + update).astype(jnp.bfloat16)

    per = row_tiles // PARTS
    rings = []
    own_news = []
    news = [news_0, news_1, news_2, news_3]
    out_copies = []
    for part in range(PARTS):

        @pl.loop(part * per, (part + 1) * per)
        def _(r):
            observed = sums[meta[8, r]] * meta[9, r].astype(jnp.float32)
            factors = users[k, x, r].astype(jnp.float32)
            gradient = observed - UNOBSERVED * coupled[r] - REGULAR * factors
            news[0][k, r] = newton(factors, gradient, ui[...])

        def piece(back, half, kk=None, part=part):
            kk = k if kk is None else kk
            if half is None:
                return news[back].at[kk, pl.ds(part * per, per)]
            return news[back].at[kk, pl.ds(part * per, per), pl.ds(half * (tile // 2), tile // 2)]

        ring = Shift(net, nx, x, along_x, piece)
        ring.send(1)
        own_news.append(sibling.hand(functools.partial(piece, 0, None)))
        rings.append(ring)
        copy = pltpu.make_async_copy(
            news[0].at[k, pl.ds(part * per, per)], unew_out.at[pl.ds(part * per, per)], local_sem.at[3 + part]
        )
        copy.start()
        out_copies.append(copy)
    mine = jnp.concatenate([items[kk, xx, y, z] for xx in range(nx) for kk in range(2)], axis=1)
    icoupled[...] = jnp.dot(mine, ug[...], preferred_element_type=jnp.float32)

    def predict_from(backs, begin, end):
        @pl.loop(0, slots, unroll=UNROLL)
        def _(i):
            row = meta[1, i]
            blocks_of_users = [news[back][kk, row] for back in backs for kk in range(2)]
            value = product(blocks_of_users, [lax.rem(x + back, nx) for back in backs], i)
            value = value if begin else predicted[i] + value
            if end:
                errors[i] = error_of(value, i)
            else:
                predicted[i] = value

    hands = own_news
    for step in range(nx // 2 + 1):
        if step > 0:
            hands = []
            for ring in rings:
                came = ring.recv(step)
                ring.send(step + 1)
                hands += pass_on(ring, came)
        for hand in hands:
            sibling.wait(hand)
        predict_from(sorted({step, (nx - step) % nx}), step == 0, step == nx // 2)

    running[...] = jnp.zeros_like(running)

    @pl.loop(0, slots, unroll=UNROLL)
    def _(i):
        added = lax.dot_general(
            errors[meta[5, i]],
            news[0][k, meta[6, i]],
            (((0,), (0,)), ((), ())),
            preferred_element_type=jnp.float32,
        )
        total = running[...] * meta[7, i].astype(jnp.float32) + added
        running[...] = total
        sums[i] = total

    @pl.loop(0, panels)
    def _(p):
        panel = sums[meta[10, p]] * meta[11, p].astype(jnp.float32)
        pair = panel.astype(jnp.bfloat16).reshape(2, owner_rows, width)
        qs[lax.div(p, nz // 2), pl.ds(2 * lax.rem(p, nz // 2), 2)] = pair

    na = ra.shape[2]
    a_rows, b_rows = pl.ds(0, na), pl.ds(na, owner_rows - na)
    b_part = Scatter(net, ny, y, along_y, lambda n, h: (n, cut(nz, h), b_rows), lambda h: (cut(nz, h),), qs, rb, yb, nz > 1)
    a_part = Scatter(net, nz, z, along_z, lambda n, h: (cut(ny, h), n, a_rows), lambda h: (cut(ny, h),), qs, ra, za, ny > 1)
    b_part.send()
    a_part.send()
    b_part.relay()
    a_part.relay()
    a_part.land()
    total = qs[:, z, a_rows].astype(jnp.float32)
    for step in a_part.steps:
        total = total + ra[step - 1].astype(jnp.float32)
    sa[...] = total.astype(jnp.bfloat16)
    c_slots = [net.slot() for _ in range(1, ny)]
    for step in range(1, ny):
        to = lax.rem(y + step, ny)
        net.push(c_slots[step - 1], sa.at[to], ta.at[step - 1], along_y(step))
    b_part.land()
    total = qs[y, :, b_rows].astype(jnp.float32)
    for step in b_part.steps:
        total = total + rb[step - 1].astype(jnp.float32)
    sb[...] = total.astype(jnp.bfloat16)
    d_slots = [net.slot() for _ in range(1, nz)]
    for step in range(1, nz):
        to = lax.rem(z + step, nz)
        net.push(d_slots[step - 1], sb.at[to], tb.at[step - 1], along_z(step))
    for step in range(1, ny):
        net.land(c_slots[step - 1], ta.at[step - 1], along_y(step))
    total_a = sa[y].astype(jnp.float32)
    for step in range(1, ny):
        total_a = total_a + ta[step - 1].astype(jnp.float32)
    for step in range(1, nz):
        net.land(d_slots[step - 1], tb.at[step - 1], along_z(step))
    total_b = sb[z].astype(jnp.float32)
    for step in range(1, nz):
        total_b = total_b + tb[step - 1].astype(jnp.float32)
    observed = jnp.concatenate([total_a, total_b], axis=0)
    factors = items[k, x, y, z].astype(jnp.float32)
    gradient = observed - UNOBSERVED * icoupled[...] - REGULAR * factors
    inew_out[...] = newton(factors, gradient, ii[...])
    for copy in out_copies:
        copy.wait()
    net.drain()


def local(nx, nz, user_factors, item_factors, ratings, tile_coords, tile_count, item_gram, user_gram, user_inverse, item_inverse):
    user_rows, width = user_factors.shape
    owner_rows = item_factors.shape[0]
    slots, tile, _ = ratings.shape
    row_tiles = user_rows // tile
    na = owner_rows // 4
    nb = owner_rows - na
    bf16, f32 = jnp.bfloat16, jnp.float32
    vmem = pl.BlockSpec(memory_space=pltpu.VMEM)
    hbm = pl.BlockSpec(memory_space=pl.ANY)
    user_new, item_new = pl.pallas_call(
        functools.partial(kernel, nx, nz),
        out_shape=(
            jax.ShapeDtypeStruct((row_tiles, tile, width), bf16),
            jax.ShapeDtypeStruct((owner_rows, width), bf16),
        ),
        in_specs=[vmem, pl.BlockSpec(memory_space=pltpu.SMEM), hbm, hbm, hbm, vmem, vmem, vmem, vmem],
        out_specs=(hbm, vmem),
        scratch_shapes=[
            pltpu.VMEM((16, 128), jnp.int32),
            pltpu.SMEM((16, 128), jnp.int32),
            pltpu.VMEM((2, nx, row_tiles, tile, width), bf16),
            pltpu.VMEM((2, nx, NY, nz, owner_rows, width), bf16),
            *[pltpu.VMEM((2, row_tiles, tile, width), bf16)] * 4,
            pltpu.VMEM((slots, tile, tile), bf16),
            pltpu.VMEM((slots, tile, tile), f32),
            pltpu.VMEM((slots, tile, tile), bf16),
            pltpu.VMEM((slots, tile, width), f32),
            pltpu.VMEM((tile, width), f32),
            pltpu.VMEM((row_tiles, tile, width), f32),
            pltpu.VMEM((owner_rows, width), f32),
            pltpu.VMEM((NY, nz, owner_rows, width), bf16),
            pltpu.VMEM((nz - 1, NY, na, width), bf16),
            pltpu.VMEM((NY, na, width), bf16),
            pltpu.VMEM((max(NY - 1, 1), na, width), bf16),
            pltpu.VMEM((max(NY - 1, 1), nz, nb, width), bf16),
            pltpu.VMEM((nz, nb, width), bf16),
            pltpu.VMEM((nz - 1, nb, width), bf16),
            pltpu.VMEM((2, max(nz // 2, 1), nb, width), bf16),
            pltpu.VMEM((2, max(NY // 2, 1), na, width), bf16),
            pltpu.SemaphoreType.DMA((SEMS,)),
            pltpu.SemaphoreType.DMA((SEMS,)),
            pltpu.SemaphoreType.DMA((4 + PARTS,)),
        ],
        compiler_params=pltpu.CompilerParams(
            collective_id=0, has_side_effects=True, vmem_limit_bytes=56 * 1024 * 1024
        ),
    )(
        tile_coords.T,
        tile_count,
        user_factors.reshape(row_tiles, tile, width),
        item_factors,
        ratings,
        item_gram.reshape(nx, 2 * width, width),
        user_gram,
        user_inverse,
        item_inverse,
    )
    return user_new.reshape(user_rows, width), item_new


def solution(mesh):
    placed = (
        P("users", "dims"),
        P("users", "dims"),
        P("users", None, None),
        P("users", None),
        P("users"),
        P(None, "dims"),
        P(None, "dims"),
        P("dims", None),
        P("dims", None),
    )
    return jax.shard_map(
        functools.partial(local, mesh.shape["dims"] // 2, mesh.shape["users"] // NY),
        mesh=mesh,
        in_specs=placed,
        out_specs=(P("users", "dims"), P("users", "dims")),
        check_vma=False,
    )
```
